256 devices in a mesh: outer: 32 (over y_lo, z, core), inner: 8 (over x, y_hi).
Axes of the slice: x: 4, y: 4 (y_hi: 2, y_lo: 2; y = y_hi * 2 + y_lo), z: 8, core: 2. Of those that a mesh axis runs over, the one named last changes fastest.
Arguments:
- queries: bfloat16 [131072, 1024], P(('outer', 'inner')), may hold values from -12 to 12
- keys: bfloat16 [131072, 1024], P(('outer', 'inner')), may hold values from -12 to 12
- values: bfloat16 [131072, 1024], P(('outer', 'inner')), may hold values from -6 to 6
Outputs:
- attended: bfloat16 [131072, 1024], P(('outer', 'inner'))
The draws below stay inside these ranges and needn't reach their ends.
All inputs are finite; a program needn't handle non-finite values.
Results may differ from the reference program's by a relative error of at most 0.0031.
Values may be sent and summed in bfloat16 or wider, within the bound.
A program may use at most 128 MiB of HBM per device.

```python
import jax
import jax.numpy as jnp
from jax import lax

DEVICE_TOKENS = 512
HEADS = 16
HEAD_SIZE = 64
WIDTH = 1024
TOKENS = 131072
SEGMENT_TOKENS_B = 4096
N_OUTER = 32
N_INNER = 8


def draw_queries(key, part):
    key = jax.random.fold_in(key, 7)
    result = jnp.clip(1.8 * jax.random.normal(key, (TOKENS, WIDTH), jnp.float32), -10.8, 10.8)
    return result.astype(jnp.bfloat16)


def draw_keys(key, part):
    key = jax.random.fold_in(key, 11)
    result = jnp.clip(1.8 * jax.random.normal(key, (TOKENS, WIDTH), jnp.float32), -10.8, 10.8)
    return result.astype(jnp.bfloat16)


def steps_of(stream_key, shape, cuts, smallest, largest):
    gain = 1.0
    for dim, blocks in cuts:
        draws = jax.random.uniform(jax.random.fold_in(jax.random.fold_in(stream_key, 6), dim), (blocks,), jnp.float32, smallest / len(cuts), largest / len(cuts))
        gain = gain * jnp.repeat(jnp.exp(draws), shape[dim] // blocks).reshape((-1,) + (1,) * (len(shape) - 1 - dim))
    return gain


def noise(key, shape, width, reach, pieces=(), kind=jnp.bfloat16):
    level = steps_of(key, shape, pieces, -0.22, 0.18) if pieces else 1.0
    values = jax.random.normal(key, shape, jnp.float32) * width * level
    return jnp.minimum(jnp.maximum(values, -reach), reach).astype(kind)


def setup_inputs(seed: int = 0) -> dict:
    splits = jax.random.split(jax.random.key(seed), 4)
    queries = draw_queries(jax.random.fold_in(splits[3], 71), 0)
    keys = draw_keys(jax.random.fold_in(splits[3], 71), 0)
    values = noise(splits[2], (TOKENS, WIDTH), 1.0, 6.0, ((0, 256),))
    return {"queries": queries, "keys": keys, "values": values}


def select_dilated(rows, stride):
    count = rows.shape[0] // stride
    shaped = rows.reshape(count, stride, HEADS, HEAD_SIZE)
    chosen = jnp.arange(stride)[:, None] == (jnp.arange(HEADS) % stride)[None, :]
    return jnp.sum(jnp.where(chosen[None, :, :, None], shaped, jnp.zeros((), rows.dtype)), axis=1)


def dense_attention(queries, keys, values):
    logit_matrix = jnp.einsum('zof,sof->ozs', queries.astype(jnp.float32), keys.astype(jnp.float32)) * (HEAD_SIZE ** -0.5)
    top = jnp.max(logit_matrix, axis=-1, keepdims=True)
    exponent_scores = jnp.exp(logit_matrix - top)
    total = jnp.sum(exponent_scores, axis=-1)
    attention_probs = exponent_scores.astype(jnp.bfloat16)
    merged_output = jnp.einsum('yeg,gyt->eyt', attention_probs.astype(jnp.float32), values.astype(jnp.float32))
    att = merged_output / jnp.transpose(total)[:, :, None]
    lse = top[..., 0] + jnp.log(total)
    return att, jnp.transpose(lse)


def spread_rows(att, lse, stride):
    count = att.shape[0]
    chosen = jnp.arange(stride)[:, None] == (jnp.arange(HEADS) % stride)[None, :]
    full_att = jnp.where(chosen[None, :, :, None], att[:, None], jnp.zeros((), jnp.float32))
    full_lse = jnp.where(chosen[None, :, :], lse[:, None], jnp.full((), -1e30, jnp.float32))
    return full_att.reshape(count * stride, HEADS, HEAD_SIZE), full_lse.reshape(count * stride, HEADS)


def merge_levels(parts):
    highest = parts[0][1]
    for pair in parts[1:]:
        highest = jnp.maximum(highest, pair[1])
    numer = jnp.zeros(parts[0][0].shape, jnp.float32)
    denom = jnp.zeros(highest.shape, jnp.float32)
    for att, lse in parts:
        weight = jnp.exp(lse - highest)
        numer = numer + weight[:, :, None] * att
        denom = denom + weight
    return numer / denom[:, :, None]


def reference(queries, keys, values):
    second_dilation = N_INNER
    third_dilation = N_OUTER * N_INNER
    gathered_query_rows = queries.reshape(TOKENS, HEADS, HEAD_SIZE)
    gathered_key_rows = keys.reshape(TOKENS, HEADS, HEAD_SIZE)
    gathered_value_rows = values.reshape(TOKENS, HEADS, HEAD_SIZE)

    def level_two(index):
        first_offset = (index * SEGMENT_TOKENS_B).astype(jnp.int32)
        segment_query = select_dilated(lax.dynamic_slice_in_dim(gathered_query_rows, first_offset, SEGMENT_TOKENS_B, 0), second_dilation)
        segment_key = select_dilated(lax.dynamic_slice_in_dim(gathered_key_rows, first_offset, SEGMENT_TOKENS_B, 0), second_dilation)
        segment_value = select_dilated(lax.dynamic_slice_in_dim(gathered_value_rows, first_offset, SEGMENT_TOKENS_B, 0), second_dilation)
        return dense_attention(segment_query, segment_key, segment_value)

    att_two, second_logsumexp = lax.map(level_two, jnp.arange(N_OUTER, dtype=jnp.int32))
    att_two = att_two.reshape(N_OUTER * DEVICE_TOKENS, HEADS, HEAD_SIZE)
    second_logsumexp = second_logsumexp.reshape(N_OUTER * DEVICE_TOKENS, HEADS)
    third_level_output, third_logsumexp = dense_attention(select_dilated(gathered_query_rows, third_dilation), select_dilated(gathered_key_rows, third_dilation), select_dilated(gathered_value_rows, third_dilation))
    second_level_rows = DEVICE_TOKENS // second_dilation
    third_level_rows = DEVICE_TOKENS // third_dilation

    def one_block(index):
        first_offset = (index * DEVICE_TOKENS).astype(jnp.int32)
        block_q = lax.dynamic_slice_in_dim(gathered_query_rows, first_offset, DEVICE_TOKENS, 0)
        block_k = lax.dynamic_slice_in_dim(gathered_key_rows, first_offset, DEVICE_TOKENS, 0)
        block_v = lax.dynamic_slice_in_dim(gathered_value_rows, first_offset, DEVICE_TOKENS, 0)
        first = dense_attention(block_q, block_k, block_v)
        second_offset = (index * second_level_rows).astype(jnp.int32)
        second = spread_rows(lax.dynamic_slice_in_dim(att_two, second_offset, second_level_rows, 0),
                             lax.dynamic_slice_in_dim(second_logsumexp, second_offset, second_level_rows, 0), second_dilation)
        third_offset = (index * third_level_rows).astype(jnp.int32)
        third = spread_rows(lax.dynamic_slice_in_dim(third_level_output, third_offset, third_level_rows, 0),
                            lax.dynamic_slice_in_dim(third_logsumexp, third_offset, third_level_rows, 0), third_dilation)
        return merge_levels([first, second, third]).astype(jnp.bfloat16)

    blocks = lax.map(one_block, jnp.arange(N_OUTER * N_INNER, dtype=jnp.int32))
    return blocks.reshape(TOKENS, WIDTH)
```

```python
import jax
import jax.numpy as jnp
from jax import lax
from jax.experimental import pallas as pl
from jax.experimental.pallas import tpu as pltpu
from jax.sharding import PartitionSpec as P

MESH = pl.DeviceIdType.MESH
F32 = jnp.float32
BF16 = jnp.bfloat16

ROWS = 512
PAIRS = 8
MID = 64
FAR = 2
INNER = 8
RG = 16
GG = 16
BACK = MID + 16
LOWEST = -1e30

INNER_STEPS = ((2, 1), (1, 1), (3, 1), (2, 0), (0, 1), (1, 0), (3, 0))
Z_STEPS = (4, 3, 5, 2, 6, 1, 7, 0)


def lane_is_second(shape):
    return lax.broadcasted_iota(jnp.int32, shape, len(shape) - 1) >= 64


def split_pair(q):
    second = lane_is_second(q.shape)
    zero = jnp.zeros((), q.dtype)
    return jnp.concatenate([jnp.where(second, zero, q), jnp.where(second, q, zero)], axis=0)


def value_block(v):
    second = lane_is_second(v.shape)
    zero = jnp.zeros((), v.dtype)
    one = jnp.ones((), v.dtype)
    first = jnp.concatenate([jnp.where(second, zero, v), jnp.where(second, zero, one)], axis=1)
    other = jnp.concatenate([jnp.where(second, v, zero), jnp.where(second, one, zero)], axis=1)
    return jnp.concatenate([first, other], axis=0)


def scores_of(q, k):
    return lax.dot_general(split_pair(q), k, (((1,), (1,)), ((), ())), preferred_element_type=F32)


def finish(s, block):
    n = s.shape[0] // 2
    top = jnp.max(s, axis=1, keepdims=True)
    prob = jnp.exp(s - top).astype(BF16)
    both = jnp.concatenate([prob[:n], prob[n:]], axis=1)
    out = jnp.dot(both, block, preferred_element_type=F32)
    total = out[:, 128:]
    second = lane_is_second((n, 128))
    return out[:, :128] / total, jnp.where(second, top[n:], top[:n]) + jnp.log(total)


def parts_of(x):
    high = x.astype(BF16)
    rest = x - high.astype(F32)
    mid = rest.astype(BF16)
    return high, mid, (rest - mid.astype(F32)).astype(BF16)


def pack_lse(lse, groups, width):
    high, mid, low = (p.astype(F32) for p in parts_of(lse))
    lane = lax.broadcasted_iota(jnp.int32, (16, 128), 1) % 64
    out = jnp.zeros((16, 128), F32)
    for g in range(groups):
        rows = slice(16 * g, 16 * g + 16)
        for t, part in enumerate((high, mid, low)):
            out = jnp.where(lane == g * width + t, part[rows], out)
    return out.astype(BF16)


def unpack_lse(packed, groups, width):
    row = lax.broadcasted_iota(jnp.int32, (128, 128), 0)
    lane = lax.broadcasted_iota(jnp.int32, (128, 128), 1)
    out = []
    for g in range(groups):
        at = row % 64 - g * width
        take = jnp.logical_and(jnp.logical_and(at >= 0, at < 3), row // 64 == lane // 64)
        out.append(jnp.dot(packed, jnp.where(take, 1.0, 0.0).astype(BF16), preferred_element_type=F32))
    return out


def wait_some(sem, count):
    @pl.when(count > 0)
    def _():
        pl.semaphore_wait(sem, count)


def kernel(
    q_hbm, k_hbm, v_hbm, out_ref,
    q_ref, k_ref, v_ref, edge, load_sem, edge_sem,
    stage, far_stage, mid_send, mid_recv, mid_ssem, mid_rsem,
    back_send, back_recv, back_ssem, back_rsem,
    kv_send, kv_recv, kv_ssem, kv_rsem,
    fq_send, fq_recv, fq_ssem, fq_rsem,
    far_send, far_recv, far_ssem, far_rsem,
    near_sem, along_sem, att_ref, lse_pair, lse_ref, far_att, far_lse,
):
    outer = lax.axis_index("outer")
    inner = lax.axis_index("inner")
    core = outer % 2
    z = (outer // 2) % 8
    y_lo = outer // 16
    x = inner // 2
    y_hi = inner % 2

    def rank(x, y_hi, y_lo, z, core):
        y = y_hi * 2 + y_lo
        hops = x - 2 * (x // 3) + y - 2 * (y // 3) + z - (z // 4) * (z - 4)
        return hops * 256 + (y_lo * 16 + z * 2 + core) * 8 + x * 2 + y_hi

    mine = rank(x, y_hi, y_lo, z, core)

    def outer_id(y_lo, z, core):
        return y_lo * 16 + z * 2 + core

    near = []
    for dc in range(2):
        for dx, dy in INNER_STEPS + ((0, 0),):
            if dc or dx or dy:
                px, py, pc = (x + dx) % 4, (y_hi + dy) % 2, (core + dc) % 2
                near.append(((outer_id(y_lo, z, pc), px * 2 + py), rank(px, py, y_lo, z, pc)))
    along = []
    for dz in Z_STEPS:
        for dy in range(2):
            if dz or dy:
                pz, py = (z + dz) % 8, (y_lo + dy) % 2
                along.append(((outer_id(py, pz, core), inner), rank(x, y_hi, py, pz, core)))

    barrier = pltpu.get_barrier_semaphore()
    lower_near = jnp.int32(0)
    lower_along = jnp.int32(0)
    for who, its in near:
        @pl.when(its > mine)
        def _(who=who):
            pl.semaphore_signal(barrier, 1, device_id=who, device_id_type=MESH)
        lower_near = lower_near + jnp.where(its < mine, 1, 0)
    for who, its in along:
        @pl.when(its > mine)
        def _(who=who):
            pl.semaphore_signal(barrier, 1, device_id=who, device_id_type=MESH)
        lower_along = lower_along + jnp.where(its < mine, 1, 0)

    edges = []
    for a, src in enumerate((q_hbm, k_hbm, v_hbm)):
        for t in range(FAR):
            copy = pltpu.make_async_copy(src.at[pl.ds(256 * t, 16), :], edge.at[a, t], edge_sem.at[a, t])
            copy.start()
            edges.append(copy)
    loads = []
    for a, (src, dst) in enumerate(((q_hbm, q_ref), (k_hbm, k_ref), (v_hbm, v_ref))):
        copy = pltpu.make_async_copy(src, dst, load_sem.at[a])
        copy.start()
        loads.append(copy)

    for copy in edges:
        copy.wait()
    row16 = lax.broadcasted_iota(jnp.int32, (16, 1024), 0)
    head16 = lax.broadcasted_iota(jnp.int32, (16, 1024), 1) // 64
    for a in range(3):
        for t in range(FAR):
            block = edge[a, t].astype(F32)
            if a == 0:
                block = block * 0.125
            picked = jnp.sum(jnp.where(row16 == head16, block, 0.0), axis=0, keepdims=True)
            for p in range(PAIRS):
                far_stage[a, pl.ds(2 * p + t, 1), :] = picked[:, 128 * p : 128 * p + 128]
    fq_send[...] = far_stage[0].astype(BF16)
    kv_send[0:16, :] = far_stage[1].astype(BF16)
    kv_send[16:32, :] = far_stage[2].astype(BF16)
    my_near = core * 8 + inner
    my_along = y_lo * 8 + z
    fq_recv[my_near] = fq_send[...]
    kv_recv[my_along] = kv_send[...]

    wait_some(barrier, lower_near + lower_along)
    for who, its in near:
        @pl.when(its < mine)
        def _(who=who):
            pl.semaphore_signal(near_sem, 1, device_id=who, device_id_type=MESH)
    for who, its in along:
        @pl.when(its < mine)
        def _(who=who):
            pl.semaphore_signal(along_sem, 1, device_id=who, device_id_type=MESH)

    def kv_copy(who):
        return pltpu.make_async_remote_copy(
            src_ref=kv_send, dst_ref=kv_recv.at[my_along], send_sem=kv_ssem, recv_sem=kv_rsem,
            device_id=who, device_id_type=MESH,
        )

    for who, its in along:
        @pl.when(its < mine)
        def _(who=who):
            kv_copy(who).start()

    for copy in loads:
        copy.wait()
    second = lane_is_second((MID, 128))

    def select_pair(p):
        first_row = (2 * p) % 8
        columns = pl.ds(pl.multiple_of(p * 128, 128), 128)
        for a, ref in enumerate((q_ref, k_ref, v_ref)):
            wide = ref[:, columns].astype(F32)
            if a == 0:
                wide = wide * 0.125
            stage[a] = wide
        for a in range(3):
            one = stage[a, pl.ds(first_row, MID, stride=8), :]
            two = stage[a, pl.ds(first_row + 1, MID, stride=8), :]
            mid_send[p, pl.ds(MID * a, MID), :] = jnp.where(second, two, one).astype(BF16)

    def pick(p, carry):
        select_pair(p)
        return carry

    lax.fori_loop(0, PAIRS, pick, 0)
    mid_recv[inner] = mid_send[inner]

    def send_near():
        wait_some(near_sem, 15 - lower_near)
        for dx, dy in INNER_STEPS:
            p = ((x + dx) % 4) * 2 + (y_hi + dy) % 2
            pltpu.make_async_remote_copy(
                src_ref=mid_send.at[p], dst_ref=mid_recv.at[inner], send_sem=mid_ssem, recv_sem=mid_rsem,
                device_id=(outer, p), device_id_type=MESH,
            ).start()
        for who, _ in near:
            pltpu.make_async_remote_copy(
                src_ref=fq_send, dst_ref=fq_recv.at[my_near], send_sem=fq_ssem, recv_sem=fq_rsem,
                device_id=who, device_id_type=MESH,
            ).start()

    def send_along():
        wait_some(along_sem, 15 - lower_along)
        for who, its in along:
            @pl.when(its > mine)
            def _(who=who):
                kv_copy(who).start()

    def middle():
        got = mid_recv.at[pl.ds(0, INNER - 1)]
        pltpu.make_async_copy(got, got, mid_rsem).wait()
        keys = mid_recv[:, MID : 2 * MID, :].reshape(ROWS, 128)
        block = value_block(mid_recv[:, 2 * MID :, :].reshape(ROWS, 128))
        for half in range(4):
            q = mid_recv[2 * half : 2 * half + 2, 0:MID, :].reshape(128, 128)
            att, lse = finish(scores_of(q, keys), block)
            for s in range(2):
                rows = slice(MID * s, MID * s + MID)
                back_send[2 * half + s, 0:MID, :] = att[rows].astype(BF16)
                back_send[2 * half + s, MID:BACK, :] = pack_lse(lse[rows], 4, 16)
        for dx, dy in INNER_STEPS:
            p = ((x + dx) % 4) * 2 + (y_hi + dy) % 2
            pltpu.make_async_remote_copy(
                src_ref=back_send.at[p], dst_ref=back_recv.at[inner], send_sem=back_ssem, recv_sem=back_rsem,
                device_id=(outer, p), device_id_type=MESH,
            ).start()
        back_recv[inner] = back_send[inner]

    def far():
        got = kv_recv.at[pl.ds(0, GG - 1)]
        pltpu.make_async_copy(got, got, kv_rsem).wait()
        got = fq_recv.at[pl.ds(0, RG - 1)]
        pltpu.make_async_copy(got, got, fq_rsem).wait()
        stage[0] = kv_recv[...].reshape(ROWS, 128).astype(F32)
        stage[1, 0:256, :] = fq_recv[...].reshape(256, 128).astype(F32)
        scores, blocks = [], []
        for p in range(PAIRS):
            q = jnp.concatenate([stage[1, pl.ds(2 * p + t, RG, stride=16), :] for t in range(FAR)], axis=0)
            k = jnp.concatenate([stage[0, pl.ds(2 * p + t, GG, stride=32), :] for t in range(FAR)], axis=0)
            v = jnp.concatenate([stage[0, pl.ds(16 + 2 * p + t, GG, stride=32), :] for t in range(FAR)], axis=0)
            scores.append(scores_of(q.astype(BF16), k.astype(BF16)))
            blocks.append(value_block(v.astype(BF16)))
        for p in range(PAIRS):
            att, lse = finish(scores[p], blocks[p])
            for t in range(FAR):
                far_att[pl.ds(2 * p + t, RG, stride=16), :] = att[RG * t : RG * t + RG]
                far_lse[pl.ds(2 * p + t, RG, stride=16), :] = lse[RG * t : RG * t + RG]
        for s in range(RG):
            far_send[s, 0:16, :] = far_att[16 * s : 16 * s + 16, :].astype(BF16)
            far_send[s, 16:32, :] = pack_lse(far_lse[16 * s : 16 * s + 16, :], 1, 16)
        for (o, i), _ in near:
            pltpu.make_async_remote_copy(
                src_ref=far_send.at[(o % 2) * 8 + i], dst_ref=far_recv.at[my_near],
                send_sem=far_ssem, recv_sem=far_rsem, device_id=(o, i), device_id_type=MESH,
            ).start()
        far_recv[my_near] = far_send[my_near]

    def first_level(p):
        columns = pl.ds(pl.multiple_of(p * 128, 128), 128)
        keys = k_ref[:, columns]
        block = value_block(v_ref[:, columns])
        for c in range(4):
            rows = pl.ds(128 * c, 128)
            q = q_ref[rows, columns] * jnp.asarray(0.125, BF16)
            att, lse = finish(scores_of(q, keys), block)
            att_ref[p, rows, :] = att
            lse_pair[rows, :] = lse
        first_row = (2 * p) % 8
        one = lse_pair[pl.ds(first_row, MID, stride=8), :]
        two = lse_pair[pl.ds(first_row + 1, MID, stride=8), :]
        lse_ref[p] = jnp.where(second, two, one)

    hops = mine // 256
    at_near = jnp.where(hops >= 6, 0, jnp.where(hops >= 3, 1, 2))
    at_along = at_near + 1
    at_mid = at_near + 3
    at_far = at_near + 5

    def step(t, carry):
        @pl.when(t == at_near)
        def _():
            send_near()

        @pl.when(t == at_along)
        def _():
            send_along()

        @pl.when(t == at_mid)
        def _():
            middle()

        @pl.when(t == at_far)
        def _():
            far()

        @pl.when(t < PAIRS)
        def _():
            first_level(t)

        return carry

    lax.fori_loop(0, PAIRS + 1, step, 0)

    got = back_recv.at[pl.ds(0, INNER - 1)]
    pltpu.make_async_copy(got, got, back_rsem).wait()
    got = far_recv.at[pl.ds(0, RG - 1)]
    pltpu.make_async_copy(got, got, far_rsem).wait()

    partial_lse = unpack_lse(far_recv[:, 16:32, :].reshape(256, 128), 1, 16)[0]
    top = partial_lse[0:16]
    for s in range(1, RG):
        top = jnp.maximum(top, partial_lse[16 * s : 16 * s + 16])
    numer = jnp.zeros((16, 128), F32)
    denom = jnp.zeros((16, 128), F32)
    for s in range(RG):
        weight = jnp.exp(partial_lse[16 * s : 16 * s + 16] - top)
        numer = numer + weight * far_recv[s, 0:16, :].astype(F32)
        denom = denom + weight
    far_att[0:16, :] = numer / denom
    far_lse[0:16, :] = top + jnp.log(denom)

    mid_lse = unpack_lse(back_recv[:, MID:BACK, :].reshape(128, 128), 4, 16)
    for p in range(PAIRS):
        first_row = (2 * p) % 8
        one = att_ref[p, pl.ds(first_row, MID, stride=8), :]
        two = att_ref[p, pl.ds(first_row + 1, MID, stride=8), :]
        att1 = jnp.where(second, two, one)
        lse1 = lse_ref[p]
        att2 = back_recv[p, 0:MID, :].astype(F32)
        lse2 = jnp.concatenate([mid_lse[g][16 * p : 16 * p + 16] for g in range(4)], axis=0)
        row = lax.broadcasted_iota(jnp.int32, (MID, 128), 0)
        att3 = jnp.zeros((MID, 128), F32)
        lse3 = jnp.full((MID, 128), LOWEST, F32)
        for t in range(FAR):
            here = row == 32 * t + p // 4
            att3 = jnp.where(here, far_att[2 * p + t : 2 * p + t + 1, :], att3)
            lse3 = jnp.where(here, far_lse[2 * p + t : 2 * p + t + 1, :], lse3)
        top = jnp.maximum(jnp.maximum(lse1, lse2), lse3)
        w1, w2, w3 = jnp.exp(lse1 - top), jnp.exp(lse2 - top), jnp.exp(lse3 - top)
        merged = (w1 * att1 + w2 * att2 + w3 * att3) / (w1 + w2 + w3)
        att_ref[p, pl.ds(first_row, MID, stride=8), :] = jnp.where(second, one, merged)
        att_ref[p, pl.ds(first_row + 1, MID, stride=8), :] = jnp.where(second, merged, two)
        out_ref[:, 128 * p : 128 * p + 128] = att_ref[p].astype(BF16)

    sent = mid_send.at[pl.ds(0, INNER - 1)]
    pltpu.make_async_copy(sent, sent, mid_ssem).wait()
    sent = back_send.at[pl.ds(0, INNER - 1)]
    pltpu.make_async_copy(sent, sent, back_ssem).wait()
    sent = kv_recv.at[pl.ds(0, GG - 1)]
    pltpu.make_async_copy(sent, sent, kv_ssem).wait()
    sent = fq_recv.at[pl.ds(0, RG - 1)]
    pltpu.make_async_copy(sent, sent, fq_ssem).wait()
    sent = far_send.at[pl.ds(0, RG - 1)]
    pltpu.make_async_copy(sent, sent, far_ssem).wait()


def on_device(queries, keys, values):
    dma = pltpu.SemaphoreType.DMA
    vmem = pltpu.VMEM
    return pl.pallas_call(
        kernel,
        out_shape=jax.ShapeDtypeStruct((ROWS, 1024), BF16),
        in_specs=[pl.BlockSpec(memory_space=pl.ANY)] * 3,
        out_specs=pl.BlockSpec(memory_space=pltpu.VMEM),
        scratch_shapes=[
            vmem((ROWS, 1024), BF16), vmem((ROWS, 1024), BF16), vmem((ROWS, 1024), BF16),
            vmem((3, FAR, 16, 1024), BF16), dma((3,)), dma((3, FAR)),
            vmem((3, ROWS, 128), F32), vmem((3, 16, 128), F32),
            vmem((INNER, 3 * MID, 128), BF16), vmem((INNER, 3 * MID, 128), BF16), dma, dma,
            vmem((INNER, BACK, 128), BF16), vmem((INNER, BACK, 128), BF16), dma, dma,
            vmem((32, 128), BF16), vmem((GG, 32, 128), BF16), dma, dma,
            vmem((16, 128), BF16), vmem((RG, 16, 128), BF16), dma, dma,
            vmem((RG, 32, 128), BF16), vmem((RG, 32, 128), BF16), dma, dma,
            pltpu.SemaphoreType.REGULAR, pltpu.SemaphoreType.REGULAR,
            vmem((PAIRS, ROWS, 128), F32), vmem((ROWS, 128), F32), vmem((PAIRS, MID, 128), F32),
            vmem((256, 128), F32), vmem((256, 128), F32),
        ],
        compiler_params=pltpu.CompilerParams(
            collective_id=0, has_side_effects=True, vmem_limit_bytes=40 * 1024 * 1024
        ),
    )(queries, keys, values)


def solution(mesh):
    spec = P(("outer", "inner"), None)
    return jax.shard_map(
        on_device, mesh=mesh, in_specs=(spec, spec, spec), out_specs=spec, check_vma=False
    )
```

```python
import jax
import jax.numpy as jnp
from jax import lax
from jax.experimental import pallas as pl
from jax.experimental.pallas import tpu as pltpu
from jax.sharding import PartitionSpec as P

MESH = pl.DeviceIdType.MESH
F32 = jnp.float32
BF16 = jnp.bfloat16

ROWS = 512
PAIRS = 8
MID = 64
FAR = 2
INNER = 8
RG = 16
GG = 16
BACK = MID + 16
LOWEST = -1e30
STORES = 8

INNER_STEPS = ((2, 2), (1, 2), (3, 2), (2, 0), (0, 2), (1, 0), (3, 0))
REST_STEPS = ((2, 1), (2, 3), (1, 1), (1, 3), (3, 1), (3, 3), (0, 1), (0, 3))
Z_STEPS = (4, 3, 5, 2, 6, 1, 7, 0)


def lane_is_second(shape):
    return lax.broadcasted_iota(jnp.int32, shape, len(shape) - 1) >= 64


def split_pair(q):
    second = lane_is_second(q.shape)
    zero = jnp.zeros((), q.dtype)
    return jnp.concatenate([jnp.where(second, zero, q), jnp.where(second, q, zero)], axis=0)


def value_block(v):
    second = lane_is_second(v.shape)
    zero = jnp.zeros((), v.dtype)
    one = jnp.ones((), v.dtype)
    first = jnp.concatenate([jnp.where(second, zero, v), jnp.where(second, zero, one)], axis=1)
    other = jnp.concatenate([jnp.where(second, v, zero), jnp.where(second, one, zero)], axis=1)
    return jnp.concatenate([first, other], axis=0)


def scores_of(q, k):
    return lax.dot_general(split_pair(q), k, (((1,), (1,)), ((), ())), preferred_element_type=F32)


def finish(s, block):
    n = s.shape[0] // 2
    top = jnp.max(s, axis=1, keepdims=True)
    prob = jnp.exp(s - top).astype(BF16)
    both = jnp.concatenate([prob[:n], prob[n:]], axis=1)
    out = jnp.dot(both, block, preferred_element_type=F32)
    total = out[:, 128:]
    second = lane_is_second((n, 128))
    return out[:, :128] / total, jnp.where(second, top[n:], top[:n]) + jnp.log(total)


def parts_of(x):
    high = x.astype(BF16)
    rest = x - high.astype(F32)
    mid = rest.astype(BF16)
    return high, mid, (rest - mid.astype(F32)).astype(BF16)


def pack_lse(lse, groups, width):
    high, mid, low = (p.astype(F32) for p in parts_of(lse))
    lane = lax.broadcasted_iota(jnp.int32, (16, 128), 1) % 64
    out = jnp.zeros((16, 128), F32)
    for g in range(groups):
        rows = slice(16 * g, 16 * g + 16)
        for t, part in enumerate((high, mid, low)):
            out = jnp.where(lane == g * width + t, part[rows], out)
    return out.astype(BF16)


def unpack_lse(packed, groups, width):
    row = lax.broadcasted_iota(jnp.int32, (128, 128), 0)
    lane = lax.broadcasted_iota(jnp.int32, (128, 128), 1)
    out = []
    for g in range(groups):
        at = row % 64 - g * width
        take = jnp.logical_and(jnp.logical_and(at >= 0, at < 3), row // 64 == lane // 64)
        out.append(jnp.dot(packed, jnp.where(take, 1.0, 0.0).astype(BF16), preferred_element_type=F32))
    return out


def wait_some(sem, count):
    @pl.when(count > 0)
    def _():
        pl.semaphore_wait(sem, count)


def kernel(
    q_hbm, k_hbm, v_hbm, out_ref,
    q_ref, k_ref, v_ref, edge, load_sem, edge_sem,
    stage, far_stage, mid_send, mid_recv, mid_ssem, mid_rsem,
    back_send, back_recv, back_ssem, back_rsem,
    kv_send, kv_recv, kv_ssem, kv_rsem,
    fq_send, fq_recv, fq_ssem, fq_rsem,
    far_send, far_recv, far_ssem, far_rsem,
    along_sem, att_ref, lse_pair, lse_ref, far_att, far_lse,
):
    outer = lax.axis_index("outer")
    inner = lax.axis_index("inner")
    core = outer % 2
    z = (outer // 2) % 8
    y_lo = outer // 16
    x = inner // 2
    y_hi = inner % 2

    y = y_hi * 2 + y_lo

    def outer_id(y_lo, z, core):
        return y_lo * 16 + z * 2 + core

    near, along = [], []
    for dx, dy in INNER_STEPS + REST_STEPS:
        px, py = (x + dx) % 4, (y + dy) % 4
        near.append((outer_id(py % 2, z, core), px * 2 + py // 2))
    wave = jnp.minimum(z, 4)
    for dz in Z_STEPS:
        for dc in range(2):
            if dz or dc:
                pz = (z + dz) % 8
                along.append(((outer_id(y_lo, pz, (core + dc) % 2), inner), jnp.minimum(pz, 4) - wave))
    early_along = jnp.where(z < 4, 2 * z + 1, 15)

    edges = []
    for a, src in ((1, k_hbm), (2, v_hbm), (0, q_hbm)):
        for t in range(FAR):
            copy = pltpu.make_async_copy(src.at[pl.ds(256 * t, 16), :], edge.at[a, t], edge_sem.at[a, t])
            copy.start()
            edges.append(copy)
    loads = []
    for a, (src, dst) in enumerate(((q_hbm, q_ref), (k_hbm, k_ref), (v_hbm, v_ref))):
        copy = pltpu.make_async_copy(src, dst, load_sem.at[a])
        copy.start()
        loads.append(copy)

    barrier = pltpu.get_barrier_semaphore()
    for who in near:
        pl.semaphore_signal(barrier, 1, device_id=who, device_id_type=MESH)
    for who, later in along:
        @pl.when(later >= 0)
        def _(who=who):
            pl.semaphore_signal(barrier, 1, device_id=who, device_id_type=MESH)

    row16 = lax.broadcasted_iota(jnp.int32, (16, 1024), 0)
    head16 = lax.broadcasted_iota(jnp.int32, (16, 1024), 1) // 64
    my_near = y * 4 + x
    my_along = z * 2 + core

    def pick_edge(a):
        for t in range(FAR):
            block = edge[a, t].astype(F32)
            picked = jnp.sum(jnp.where(row16 == head16, block, 0.0), axis=0, keepdims=True)
            for p in range(PAIRS):
                far_stage[a, pl.ds(2 * p + t, 1), :] = picked[:, 128 * p : 128 * p + 128]

    def kv_copy(who):
        return pltpu.make_async_remote_copy(
            src_ref=kv_send, dst_ref=kv_recv.at[my_along], send_sem=kv_ssem, recv_sem=kv_rsem,
            device_id=who, device_id_type=MESH,
        )

    def fq_copy(who):
        return pltpu.make_async_remote_copy(
            src_ref=fq_send, dst_ref=fq_recv.at[my_near], send_sem=fq_ssem, recv_sem=fq_rsem,
            device_id=who, device_id_type=MESH,
        )

    def mid_copy(who):
        return pltpu.make_async_remote_copy(
            src_ref=mid_send.at[who[1]], dst_ref=mid_recv.at[inner], send_sem=mid_ssem, recv_sem=mid_rsem,
            device_id=who, device_id_type=MESH,
        )

    for copy in edges[:4]:
        copy.wait()
    pick_edge(1)
    pick_edge(2)
    kv_send[0:16, :] = far_stage[1].astype(BF16)
    kv_send[16:32, :] = far_stage[2].astype(BF16)
    kv_recv[my_along] = kv_send[...]
    for copy in edges[4:]:
        copy.wait()
    pick_edge(0)
    fq_send[...] = (far_stage[0] * 0.125).astype(BF16)
    fq_recv[my_near] = fq_send[...]

    second = lane_is_second((MID, 128))

    def pick(p, carry):
        first_row = (2 * p) % 8
        columns = pl.ds(pl.multiple_of(p * 128, 128), 128)
        for a, ref in enumerate((q_ref, k_ref, v_ref)):
            wide = ref[:, columns].astype(F32)
            if a == 0:
                wide = wide * 0.125
            stage[a] = wide
        for a in range(3):
            one = stage[a, pl.ds(first_row, MID, stride=8), :]
            two = stage[a, pl.ds(first_row + 1, MID, stride=8), :]
            mid_send[p, pl.ds(MID * a, MID), :] = jnp.where(second, two, one).astype(BF16)
        return carry


    def pick_all():
        for copy in loads:
            copy.wait()
        lax.fori_loop(0, PAIRS, pick, 0)
        mid_recv[inner] = mid_send[inner]

    def meet():
        pl.semaphore_wait(barrier, 15 + early_along)
        for who, later in along:
            @pl.when(later <= 0)
            def _(who=who):
                kv_copy(who).start()
        for who, later in along:
            @pl.when(later < 0)
            def _(who=who):
                pl.semaphore_signal(along_sem, 1, device_id=who, device_id_type=MESH)
        for who in near:
            fq_copy(who).start()

    def send_mid():
        for who in near[:7]:
            mid_copy(who).start()

    def send_along():
        wait_some(along_sem, 15 - early_along)
        for who, later in along:
            @pl.when(later > 0)
            def _(who=who):
                kv_copy(who).start()

    def middle():
        got = mid_recv.at[pl.ds(0, INNER - 1)]
        pltpu.make_async_copy(got, got, mid_rsem).wait()
        keys = mid_recv[:, MID : 2 * MID, :].reshape(ROWS, 128)
        block = value_block(mid_recv[:, 2 * MID :, :].reshape(ROWS, 128))
        for n in range(4):
            q = mid_recv[2 * n : 2 * n + 2, 0:MID, :].reshape(2 * MID, 128)
            att, lse = finish(scores_of(q, keys), block)
            for s in range(2):
                rows = slice(MID * s, MID * s + MID)
                back_send[2 * n + s, 0:MID, :] = att[rows].astype(BF16)
                back_send[2 * n + s, MID:BACK, :] = pack_lse(lse[rows], 4, 16)
        for who in near[:7]:
            pltpu.make_async_remote_copy(
                src_ref=back_send.at[who[1]], dst_ref=back_recv.at[inner], send_sem=back_ssem, recv_sem=back_rsem,
                device_id=who, device_id_type=MESH,
            ).start()
        back_recv[inner] = back_send[inner]

    def far():
        got = kv_recv.at[pl.ds(0, GG - 1)]
        pltpu.make_async_copy(got, got, kv_rsem).wait()
        got = fq_recv.at[pl.ds(0, RG - 1)]
        pltpu.make_async_copy(got, got, fq_rsem).wait()
        stage[0] = kv_recv[...].reshape(ROWS, 128).astype(F32)
        stage[1, 0:256, :] = fq_recv[...].reshape(256, 128).astype(F32)
        scores, blocks = [], []
        for p in range(PAIRS):
            q = jnp.concatenate([stage[1, pl.ds(2 * p + t, RG, stride=16), :] for t in range(FAR)], axis=0)
            k = jnp.concatenate([stage[0, pl.ds(2 * p + t, GG, stride=32), :] for t in range(FAR)], axis=0)
            v = jnp.concatenate([stage[0, pl.ds(16 + 2 * p + t, GG, stride=32), :] for t in range(FAR)], axis=0)
            scores.append(scores_of(q.astype(BF16), k.astype(BF16)))
            blocks.append(value_block(v.astype(BF16)))
        for p in range(PAIRS):
            att, lse = finish(scores[p], blocks[p])
            for t in range(FAR):
                far_att[pl.ds(2 * p + t, RG, stride=16), :] = att[RG * t : RG * t + RG]
                far_lse[pl.ds(2 * p + t, RG, stride=16), :] = lse[RG * t : RG * t + RG]
        for s in range(RG):
            far_send[s, 0:16, :] = far_att[16 * s : 16 * s + 16, :].astype(BF16)
            far_send[s, 16:32, :] = pack_lse(far_lse[16 * s : 16 * s + 16, :], 1, 16)
        for who in near:
            its_y = who[1] % 2 * 2 + who[0] // 16
            pltpu.make_async_remote_copy(
                src_ref=far_send.at[its_y * 4 + who[1] // 2], dst_ref=far_recv.at[my_near],
                send_sem=far_ssem, recv_sem=far_rsem, device_id=who, device_id_type=MESH,
            ).start()
        far_recv[my_near] = far_send[my_near]

    def first_level(p):
        columns = pl.ds(pl.multiple_of(p * 128, 128), 128)
        keys = k_ref[:, columns]
        block = value_block(v_ref[:, columns])
        for c in range(4):
            rows = pl.ds(128 * c, 128)
            q = q_ref[rows, columns] * jnp.asarray(0.125, BF16)
            att, lse = finish(scores_of(q, keys), block)
            att_ref[p, rows, :] = att
            lse_pair[rows, :] = lse
        first_row = (2 * p) % 8
        one = lse_pair[pl.ds(first_row, MID, stride=8), :]
        two = lse_pair[pl.ds(first_row + 1, MID, stride=8), :]
        lse_ref[p] = jnp.where(second, two, one)

    near_hops = x - 2 * (x // 3) + y - 2 * (y // 3)
    opens = jnp.where(near_hops >= 3, 0, 3 - near_hops)
    events = (
        (opens, meet),
        (0, pick_all),
        (jnp.maximum(opens, 1), send_mid),
        (jnp.where(z < 4, 8 - wave - near_hops // 2, 1), send_along),
        (9 - near_hops // 2, far),
        (9 - near_hops // 2, middle),
    )

    def step(t, carry):
        for at, event in events:
            @pl.when(t == at)
            def _(event=event):
                event()

        @pl.when(jnp.logical_and(t > 0, t <= PAIRS))
        def _():
            first_level(t - 1)

        return carry

    lax.fori_loop(0, PAIRS + 2, step, 0)

    got = back_recv.at[pl.ds(0, INNER - 1)]
    pltpu.make_async_copy(got, got, back_rsem).wait()
    got = far_recv.at[pl.ds(0, RG - 1)]
    pltpu.make_async_copy(got, got, far_rsem).wait()

    partial_lse = unpack_lse(far_recv[:, 16:32, :].reshape(256, 128), 1, 16)[0]
    top = partial_lse[0:16]
    for s in range(1, RG):
        top = jnp.maximum(top, partial_lse[16 * s : 16 * s + 16])
    numer = jnp.zeros((16, 128), F32)
    denom = jnp.zeros((16, 128), F32)
    for s in range(RG):
        weight = jnp.exp(partial_lse[16 * s : 16 * s + 16] - top)
        numer = numer + weight * far_recv[s, 0:16, :].astype(F32)
        denom = denom + weight
    far_att[0:16, :] = numer / denom
    far_lse[0:16, :] = top + jnp.log(denom)

    mid_lse = unpack_lse(back_recv[:, MID:BACK, :].reshape(128, 128), 4, 16)
    for p in range(PAIRS):
        first_row = (2 * p) % 8
        one = att_ref[p, pl.ds(first_row, MID, stride=8), :]
        two = att_ref[p, pl.ds(first_row + 1, MID, stride=8), :]
        att1 = jnp.where(second, two, one)
        lse1 = lse_ref[p]
        att2 = back_recv[p, 0:MID, :].astype(F32)
        lse2 = jnp.concatenate([mid_lse[g][16 * p : 16 * p + 16] for g in range(4)], axis=0)
        row = lax.broadcasted_iota(jnp.int32, (MID, 128), 0)
        att3 = jnp.zeros((MID, 128), F32)
        lse3 = jnp.full((MID, 128), LOWEST, F32)
        for t in range(FAR):
            here = row == 32 * t + p // 4
            att3 = jnp.where(here, far_att[2 * p + t : 2 * p + t + 1, :], att3)
            lse3 = jnp.where(here, far_lse[2 * p + t : 2 * p + t + 1, :], lse3)
        top = jnp.maximum(jnp.maximum(lse1, lse2), lse3)
        w1, w2, w3 = jnp.exp(lse1 - top), jnp.exp(lse2 - top), jnp.exp(lse3 - top)
        merged = (w1 * att1 + w2 * att2 + w3 * att3) / (w1 + w2 + w3)
        att_ref[p, pl.ds(first_row, MID, stride=8), :] = jnp.where(second, one, merged)
        att_ref[p, pl.ds(first_row + 1, MID, stride=8), :] = jnp.where(second, merged, two)
        out_ref[:, 128 * p : 128 * p + 128] = att_ref[p].astype(BF16)

    sent = mid_send.at[pl.ds(0, INNER - 1)]
    pltpu.make_async_copy(sent, sent, mid_ssem).wait()
    sent = back_send.at[pl.ds(0, INNER - 1)]
    pltpu.make_async_copy(sent, sent, back_ssem).wait()
    sent = kv_recv.at[pl.ds(0, GG - 1)]
    pltpu.make_async_copy(sent, sent, kv_ssem).wait()
    sent = fq_recv.at[pl.ds(0, RG - 1)]
    pltpu.make_async_copy(sent, sent, fq_ssem).wait()
    sent = far_send.at[pl.ds(0, RG - 1)]
    pltpu.make_async_copy(sent, sent, far_ssem).wait()


def store(merged_ref, out_hbm, sem):
    rows = ROWS // STORES
    copies = []
    for n in range(STORES):
        part = pl.ds(rows * n, rows)
        copies.append(pltpu.make_async_copy(merged_ref.at[part, :], out_hbm.at[part, :], sem.at[n]))
    for copy in copies:
        copy.start()
    for copy in copies:
        copy.wait()


def on_device(queries, keys, values):
    dma = pltpu.SemaphoreType.DMA
    vmem = pltpu.VMEM
    merged = pl.pallas_call(
        kernel,
        out_shape=pltpu.VMEM((ROWS, 1024), BF16),
        in_specs=[pl.BlockSpec(memory_space=pltpu.HBM)] * 3,
        out_specs=pl.BlockSpec(memory_space=pltpu.VMEM),
        scratch_shapes=[
            vmem((ROWS, 1024), BF16), vmem((ROWS, 1024), BF16), vmem((ROWS, 1024), BF16),
            vmem((3, FAR, 16, 1024), BF16), dma((3,)), dma((3, FAR)),
            vmem((3, ROWS, 128), F32), vmem((3, 16, 128), F32),
            vmem((INNER, 3 * MID, 128), BF16), vmem((INNER, 3 * MID, 128), BF16), dma, dma,
            vmem((INNER, BACK, 128), BF16), vmem((INNER, BACK, 128), BF16), dma, dma,
            vmem((32, 128), BF16), vmem((GG, 32, 128), BF16), dma, dma,
            vmem((16, 128), BF16), vmem((RG, 16, 128), BF16), dma, dma,
            vmem((RG, 32, 128), BF16), vmem((RG, 32, 128), BF16), dma, dma,
            pltpu.SemaphoreType.REGULAR,
            vmem((PAIRS, ROWS, 128), F32), vmem((ROWS, 128), F32), vmem((PAIRS, MID, 128), F32),
            vmem((256, 128), F32), vmem((256, 128), F32),
        ],
        compiler_params=pltpu.CompilerParams(
            collective_id=0, has_side_effects=True, vmem_limit_bytes=40 * 1024 * 1024
        ),
    )(*(pltpu.with_memory_space_constraint(a, pltpu.HBM) for a in (queries, keys, values)))
    return pl.pallas_call(
        store,
        out_shape=pltpu.HBM((ROWS, 1024), BF16),
        in_specs=[pl.BlockSpec(memory_space=pltpu.VMEM)],
        out_specs=pl.BlockSpec(memory_space=pltpu.HBM),
        scratch_shapes=[dma((STORES,))],
    )(pltpu.with_memory_space_constraint(merged, pltpu.VMEM))


def solution(mesh):
    spec = P(("outer", "inner"), None)
    return jax.shard_map(
        on_device, mesh=mesh, in_specs=(spec, spec, spec), out_specs=spec, check_vma=False
    )
```

```python
import jax
import jax.numpy as jnp
from jax import lax
from jax.experimental import pallas as pl
from jax.experimental.pallas import tpu as pltpu
from jax.sharding import PartitionSpec as P

MESH = pl.DeviceIdType.MESH
F32 = jnp.float32
BF16 = jnp.bfloat16

ROWS = 512
PAIRS = 8
MID = 64
FAR = 2
INNER = 8
RG = 16
GG = 16
BACK = MID + 16
LOWEST = -1e30

INNER_STEPS = ((2, 2), (1, 2), (3, 2), (2, 0), (0, 2), (1, 0), (3, 0))
REST_STEPS = ((2, 1), (2, 3), (1, 1), (1, 3), (3, 1), (3, 3), (0, 1), (0, 3))
Z_STEPS = (4, 3, 5, 2, 6, 1, 7, 0)


def lane_is_second(shape):
    return lax.broadcasted_iota(jnp.int32, shape, len(shape) - 1) >= 64


def split_pair(q):
    second = lane_is_second(q.shape)
    zero = jnp.zeros((), q.dtype)
    return jnp.concatenate([jnp.where(second, zero, q), jnp.where(second, q, zero)], axis=0)


def value_block(v):
    second = lane_is_second(v.shape)
    zero = jnp.zeros((), v.dtype)
    one = jnp.ones((), v.dtype)
    first = jnp.concatenate([jnp.where(second, zero, v), jnp.where(second, zero, one)], axis=1)
    other = jnp.concatenate([jnp.where(second, v, zero), jnp.where(second, one, zero)], axis=1)
    return jnp.concatenate([first, other], axis=0)


def scores_of(q, k):
    return lax.dot_general(split_pair(q), k, (((1,), (1,)), ((), ())), preferred_element_type=F32)


def finish(s, block):
    n = s.shape[0] // 2
    top = jnp.max(s, axis=1, keepdims=True)
    prob = jnp.exp(s - top).astype(BF16)
    both = jnp.concatenate([prob[:n], prob[n:]], axis=1)
    out = jnp.dot(both, block, preferred_element_type=F32)
    total = out[:, 128:]
    second = lane_is_second((n, 128))
    return out[:, :128] / total, jnp.where(second, top[n:], top[:n]) + jnp.log(total)


def parts_of(x):
    high = x.astype(BF16)
    rest = x - high.astype(F32)
    mid = rest.astype(BF16)
    return high, mid, (rest - mid.astype(F32)).astype(BF16)


def pack_lse(lse, groups, width):
    high, mid, low = (p.astype(F32) for p in parts_of(lse))
    lane = lax.broadcasted_iota(jnp.int32, (16, 128), 1) % 64
    out = jnp.zeros((16, 128), F32)
    for g in range(groups):
        rows = slice(16 * g, 16 * g + 16)
        for t, part in enumerate((high, mid, low)):
            out = jnp.where(lane == g * width + t, part[rows], out)
    return out.astype(BF16)


def unpack_lse(packed, groups, width):
    row = lax.broadcasted_iota(jnp.int32, (128, 128), 0)
    lane = lax.broadcasted_iota(jnp.int32, (128, 128), 1)
    out = []
    for g in range(groups):
        at = row % 64 - g * width
        take = jnp.logical_and(jnp.logical_and(at >= 0, at < 3), row // 64 == lane // 64)
        out.append(jnp.dot(packed, jnp.where(take, 1.0, 0.0).astype(BF16), preferred_element_type=F32))
    return out


def kernel(
    q_hbm, k_hbm, v_hbm, merged_ref, two_ref, far_recv,
    q_ref, k_ref, v_ref, edge, load_sem, edge_sem,
    stage, far_stage, mid_send, mid_recv, mid_ssem, mid_rsem,
    back_send, back_recv, back_ssem, back_rsem,
    kv_send, kv_recv, kv_ssem, kv_rsem,
    fq_send, fq_recv, fq_ssem, fq_rsem,
    far_send, far_ssem, far_rsem,
    along_sem, att_ref, lse_pair, lse_ref, far_att, far_lse,
):
    outer = lax.axis_index("outer")
    inner = lax.axis_index("inner")
    core = outer % 2
    z = (outer // 2) % 8
    y_lo = outer // 16
    x = inner // 2
    y_hi = inner % 2

    y = y_hi * 2 + y_lo

    def outer_id(y_lo, z, core):
        return y_lo * 16 + z * 2 + core

    near, along = [], []
    for dx, dy in INNER_STEPS + REST_STEPS:
        px, py = (x + dx) % 4, (y + dy) % 4
        near.append((outer_id(py % 2, z, core), px * 2 + py // 2))
    wave = jnp.minimum(z, 4)
    for dz in Z_STEPS:
        for dc in range(2):
            if dz or dc:
                pz = (z + dz) % 8
                along.append(((outer_id(y_lo, pz, (core + dc) % 2), inner), jnp.minimum(pz, 4) - wave, pz))
    early_along = jnp.where(z < 4, 2 * z + 1, 15)

    entry = sum(9 * v - 2 * (v // 2) - 11 * (v // 3) for v in (x, y))
    opens = jnp.where(entry < 24, 1, 0)
    at_mid = 7 + opens
    at_far = at_mid + jnp.where(entry < 5, 1, 0)
    at_along_early = jnp.where(z < 3, 4 + opens - z, -1)
    at_along_late = jnp.where(z < 4, at_mid - jnp.where(z == 0, 0, wave) + wave // 3, -1)

    edges = []
    for a, src in ((1, k_hbm), (2, v_hbm), (0, q_hbm)):
        for t in range(FAR):
            copy = pltpu.make_async_copy(src.at[pl.ds(256 * t, 16), :], edge.at[a, t], edge_sem.at[a, t])
            copy.start()
            edges.append(copy)
    loads = []
    for a, (src, dst) in enumerate(((q_hbm, q_ref), (k_hbm, k_ref), (v_hbm, v_ref))):
        copy = pltpu.make_async_copy(src, dst, load_sem.at[a])
        copy.start()
        loads.append(copy)

    barrier = pltpu.get_barrier_semaphore()
    for who in near:
        pl.semaphore_signal(barrier, 1, device_id=who, device_id_type=MESH)
    for who, later, _ in along:
        @pl.when(later >= 0)
        def _(who=who):
            pl.semaphore_signal(barrier, 1, device_id=who, device_id_type=MESH)

    row16 = lax.broadcasted_iota(jnp.int32, (16, 1024), 0)
    head16 = lax.broadcasted_iota(jnp.int32, (16, 1024), 1) // 64
    my_near = y * 4 + x
    my_along = z * 2 + core

    def pick_edge(a):
        for t in range(FAR):
            block = edge[a, t].astype(F32)
            picked = jnp.sum(jnp.where(row16 == head16, block, 0.0), axis=0, keepdims=True)
            for p in range(PAIRS):
                far_stage[a, pl.ds(2 * p + t, 1), :] = picked[:, 128 * p : 128 * p + 128]

    def kv_copy(who):
        return pltpu.make_async_remote_copy(
            src_ref=kv_send, dst_ref=kv_recv.at[my_along], send_sem=kv_ssem, recv_sem=kv_rsem,
            device_id=who, device_id_type=MESH,
        )

    def fq_copy(who):
        return pltpu.make_async_remote_copy(
            src_ref=fq_send, dst_ref=fq_recv.at[my_near], send_sem=fq_ssem, recv_sem=fq_rsem,
            device_id=who, device_id_type=MESH,
        )

    def mid_copy(who):
        return pltpu.make_async_remote_copy(
            src_ref=mid_send.at[who[1]], dst_ref=mid_recv.at[inner], send_sem=mid_ssem, recv_sem=mid_rsem,
            device_id=who, device_id_type=MESH,
        )

    for copy in edges[:4]:
        copy.wait()
    pick_edge(1)
    pick_edge(2)
    kv_send[0:16, :] = far_stage[1].astype(BF16)
    kv_send[16:32, :] = far_stage[2].astype(BF16)
    kv_recv[my_along] = kv_send[...]
    for copy in edges[4:]:
        copy.wait()
    pick_edge(0)
    fq_send[...] = (far_stage[0] * 0.125).astype(BF16)
    fq_recv[my_near] = fq_send[...]

    second = lane_is_second((MID, 128))

    def pick(p):
        first_row = (2 * p) % 8
        columns = pl.ds(pl.multiple_of(p * 128, 128), 128)
        for a, ref in enumerate((q_ref, k_ref, v_ref)):
            wide = ref[:, columns].astype(F32)
            if a == 0:
                wide = wide * 0.125
            stage[a] = wide
        for a in range(3):
            one = stage[a, pl.ds(first_row, MID, stride=8), :]
            two = stage[a, pl.ds(first_row + 1, MID, stride=8), :]
            mid_send[p, pl.ds(MID * a, MID), :] = jnp.where(second, two, one).astype(BF16)


    def pick_all():
        for copy in loads:
            copy.wait()
        for who in near[:7]:
            pick(who[1])

            @pl.when(opens == 0)
            def _(who=who):
                mid_copy(who).start()
        pick(inner)
        mid_recv[inner] = mid_send[inner]

    def meet():
        pl.semaphore_wait(barrier, 15 + early_along)
        for who, later, _ in along:
            @pl.when(later < 0)
            def _(who=who):
                kv_copy(who).start()
        for who, later, _ in along:
            @pl.when(later < 0)
            def _(who=who):
                pl.semaphore_signal(along_sem.at[jnp.where(z < 4, 0, 1)], 1, device_id=who, device_id_type=MESH)
        for who, later, _ in along:
            @pl.when(later == 0)
            def _(who=who):
                kv_copy(who).start()
        for who in near:
            fq_copy(who).start()

    def send_mid():
        for who in near[:7]:
            mid_copy(who).start()

    def send_along_early():
        pl.semaphore_wait(along_sem.at[0], 6 - 2 * z)
        for who, later, pz in along:
            @pl.when(jnp.logical_and(later > 0, pz < 4))
            def _(who=who):
                kv_copy(who).start()

    def send_along_late():
        pl.semaphore_wait(along_sem.at[1], 8)
        for who, later, pz in along:
            @pl.when(jnp.logical_and(later > 0, pz >= 4))
            def _(who=who):
                kv_copy(who).start()

    def middle():
        got = mid_recv.at[pl.ds(0, INNER - 1)]
        pltpu.make_async_copy(got, got, mid_rsem).wait()
        keys = mid_recv[:, MID : 2 * MID, :].reshape(ROWS, 128)
        block = value_block(mid_recv[:, 2 * MID :, :].reshape(ROWS, 128))
        for n in range(4):
            q = mid_recv[2 * n : 2 * n + 2, 0:MID, :].reshape(2 * MID, 128)
            att, lse = finish(scores_of(q, keys), block)
            for s in range(2):
                rows = slice(MID * s, MID * s + MID)
                back_send[2 * n + s, 0:MID, :] = att[rows].astype(BF16)
                back_send[2 * n + s, MID:BACK, :] = pack_lse(lse[rows], 4, 16)
        for who in near[:7]:
            pltpu.make_async_remote_copy(
                src_ref=back_send.at[who[1]], dst_ref=back_recv.at[inner], send_sem=back_ssem, recv_sem=back_rsem,
                device_id=who, device_id_type=MESH,
            ).start()
        back_recv[inner] = back_send[inner]

    def far():
        got = kv_recv.at[pl.ds(0, GG - 1)]
        pltpu.make_async_copy(got, got, kv_rsem).wait()
        got = fq_recv.at[pl.ds(0, RG - 1)]
        pltpu.make_async_copy(got, got, fq_rsem).wait()
        stage[0] = kv_recv[...].reshape(ROWS, 128).astype(F32)
        stage[1, 0:256, :] = fq_recv[...].reshape(256, 128).astype(F32)
        scores, blocks = [], []
        for p in range(PAIRS):
            q = jnp.concatenate([stage[1, pl.ds(2 * p + t, RG, stride=16), :] for t in range(FAR)], axis=0)
            k = jnp.concatenate([stage[0, pl.ds(2 * p + t, GG, stride=32), :] for t in range(FAR)], axis=0)
            v = jnp.concatenate([stage[0, pl.ds(16 + 2 * p + t, GG, stride=32), :] for t in range(FAR)], axis=0)
            scores.append(scores_of(q.astype(BF16), k.astype(BF16)))
            blocks.append(value_block(v.astype(BF16)))
        for p in range(PAIRS):
            att, lse = finish(scores[p], blocks[p])
            for t in range(FAR):
                far_att[pl.ds(2 * p + t, RG, stride=16), :] = att[RG * t : RG * t + RG]
                far_lse[pl.ds(2 * p + t, RG, stride=16), :] = lse[RG * t : RG * t + RG]
        for s in range(RG):
            far_send[s, 0:16, :] = far_att[16 * s : 16 * s + 16, :].astype(BF16)
            far_send[s, 16:32, :] = pack_lse(far_lse[16 * s : 16 * s + 16, :], 1, 16)
        for who in near:
            its_y = who[1] % 2 * 2 + who[0] // 16
            pltpu.make_async_remote_copy(
                src_ref=far_send.at[its_y * 4 + who[1] // 2], dst_ref=far_recv.at[my_near],
                send_sem=far_ssem, recv_sem=far_rsem, device_id=who, device_id_type=MESH,
            ).start()
        far_recv[my_near] = far_send[my_near]

    def first_level(p):
        columns = pl.ds(pl.multiple_of(p * 128, 128), 128)
        keys = k_ref[:, columns]
        block = value_block(v_ref[:, columns])
        for c in range(4):
            rows = pl.ds(128 * c, 128)
            q = q_ref[rows, columns] * jnp.asarray(0.125, BF16)
            att, lse = finish(scores_of(q, keys), block)
            att_ref[p, rows, :] = att
            lse_pair[rows, :] = lse
        first_row = (2 * p) % 8
        one = lse_pair[pl.ds(first_row, MID, stride=8), :]
        two = lse_pair[pl.ds(first_row + 1, MID, stride=8), :]
        lse_ref[p] = jnp.where(second, two, one)

    events = (
        (opens, meet),
        (0, pick_all),
        (jnp.where(opens > 0, opens, -1), send_mid),
        (at_along_early, send_along_early),
        (at_along_late, send_along_late),
        (at_mid, middle),
        (at_far, far),
    )

    def step(t, carry):
        for at, event in events:
            @pl.when(t == at)
            def _(event=event):
                event()

        @pl.when(jnp.logical_and(t > 0, t <= PAIRS))
        def _():
            first_level(t - 1)

        return carry

    lax.fori_loop(0, PAIRS + 2, step, 0)

    got = back_recv.at[pl.ds(0, INNER - 1)]
    pltpu.make_async_copy(got, got, back_rsem).wait()
    mid_lse = unpack_lse(back_recv[:, MID:BACK, :].reshape(128, 128), 4, 16)
    for p in range(PAIRS):
        first_row = (2 * p) % 8
        one = att_ref[p, pl.ds(first_row, MID, stride=8), :]
        two = att_ref[p, pl.ds(first_row + 1, MID, stride=8), :]
        lse1 = lse_ref[p]
        lse2 = jnp.concatenate([mid_lse[g][16 * p : 16 * p + 16] for g in range(4)], axis=0)
        top = jnp.maximum(lse1, lse2)
        w1, w2 = jnp.exp(lse1 - top), jnp.exp(lse2 - top)
        total = w1 + w2
        merged = (w1 * jnp.where(second, two, one) + w2 * back_recv[p, 0:MID, :].astype(F32)) / total
        lse = top + jnp.log(total)
        for t in range(FAR):
            row = 32 * t + p // 4
            two_ref[0, 2 * p + t : 2 * p + t + 1, :] = merged[row : row + 1]
            two_ref[1, 2 * p + t : 2 * p + t + 1, :] = lse[row : row + 1]
        att_ref[p, pl.ds(first_row, MID, stride=8), :] = jnp.where(second, one, merged)
        att_ref[p, pl.ds(first_row + 1, MID, stride=8), :] = jnp.where(second, merged, two)
        merged_ref[:, 128 * p : 128 * p + 128] = att_ref[p].astype(BF16)

    got = far_recv.at[pl.ds(0, RG - 1)]
    pltpu.make_async_copy(got, got, far_rsem).wait()

    sent = mid_send.at[pl.ds(0, INNER - 1)]
    pltpu.make_async_copy(sent, sent, mid_ssem).wait()
    sent = back_send.at[pl.ds(0, INNER - 1)]
    pltpu.make_async_copy(sent, sent, back_ssem).wait()
    sent = kv_recv.at[pl.ds(0, GG - 1)]
    pltpu.make_async_copy(sent, sent, kv_ssem).wait()
    sent = fq_recv.at[pl.ds(0, RG - 1)]
    pltpu.make_async_copy(sent, sent, fq_ssem).wait()
    sent = far_send.at[pl.ds(0, RG - 1)]
    pltpu.make_async_copy(sent, sent, far_ssem).wait()


def merge(merged_ref, two_ref, far_recv, out_hbm, edge, sem):
    copies = []
    for t in range(FAR):
        rest = pl.ds(256 * t + 16, 240)
        copies.append(pltpu.make_async_copy(merged_ref.at[rest, :], out_hbm.at[rest, :], sem.at[t]))
        copies[t].start()

    partial_lse = unpack_lse(far_recv[:, 16:32, :].reshape(256, 128), 1, 16)[0]
    top = two_ref[1]
    for s in range(RG):
        top = jnp.maximum(top, partial_lse[16 * s : 16 * s + 16])
    weight = jnp.exp(two_ref[1] - top)
    numer = weight * two_ref[0]
    denom = weight
    for s in range(RG):
        weight = jnp.exp(partial_lse[16 * s : 16 * s + 16] - top)
        numer = numer + weight * far_recv[s, 0:16, :].astype(F32)
        denom = denom + weight
    result = numer / denom

    row = lax.broadcasted_iota(jnp.int32, (16, 128), 0)
    half = lax.broadcasted_iota(jnp.int32, (16, 128), 1) // 64
    for t in range(FAR):
        for p in range(PAIRS):
            columns = slice(128 * p, 128 * p + 128)
            old = merged_ref[256 * t : 256 * t + 16, columns].astype(F32)
            new = jnp.where(row == 2 * p + half, result[2 * p + t : 2 * p + t + 1], old)
            edge[t, :, columns] = new.astype(BF16)
        copies.append(pltpu.make_async_copy(edge.at[t], out_hbm.at[pl.ds(256 * t, 16), :], sem.at[FAR + t]))
        copies[FAR + t].start()
    for copy in copies:
        copy.wait()


def on_device(queries, keys, values):
    dma = pltpu.SemaphoreType.DMA
    vmem = pltpu.VMEM
    results = pl.pallas_call(
        kernel,
        out_shape=[
            vmem((ROWS, 1024), BF16), vmem((2, 16, 128), F32), vmem((RG, 32, 128), BF16),
        ],
        in_specs=[pl.BlockSpec(memory_space=pltpu.HBM)] * 3,
        out_specs=[pl.BlockSpec(memory_space=pltpu.VMEM)] * 3,
        scratch_shapes=[
            vmem((ROWS, 1024), BF16), vmem((ROWS, 1024), BF16), vmem((ROWS, 1024), BF16),
            vmem((3, FAR, 16, 1024), BF16), dma((3,)), dma((3, FAR)),
            vmem((3, ROWS, 128), F32), vmem((3, 16, 128), F32),
            vmem((INNER, 3 * MID, 128), BF16), vmem((INNER, 3 * MID, 128), BF16), dma, dma,
            vmem((INNER, BACK, 128), BF16), vmem((INNER, BACK, 128), BF16), dma, dma,
            vmem((32, 128), BF16), vmem((GG, 32, 128), BF16), dma, dma,
            vmem((16, 128), BF16), vmem((RG, 16, 128), BF16), dma, dma,
            vmem((RG, 32, 128), BF16), dma, dma,
            pltpu.SemaphoreType.REGULAR((2,)),
            vmem((PAIRS, ROWS, 128), F32), vmem((ROWS, 128), F32), vmem((PAIRS, MID, 128), F32),
            vmem((256, 128), F32), vmem((256, 128), F32),
        ],
        compiler_params=pltpu.CompilerParams(
            collective_id=0, has_side_effects=True, vmem_limit_bytes=40 * 1024 * 1024
        ),
    )(*(pltpu.with_memory_space_constraint(a, pltpu.HBM) for a in (queries, keys, values)))
    return pl.pallas_call(
        merge,
        out_shape=pltpu.HBM((ROWS, 1024), BF16),
        in_specs=[pl.BlockSpec(memory_space=pltpu.VMEM)] * 3,
        out_specs=pl.BlockSpec(memory_space=pltpu.HBM),
        scratch_shapes=[
            vmem((FAR, 16, 1024), BF16), dma((2 * FAR,)),
        ],
        compiler_params=pltpu.CompilerParams(vmem_limit_bytes=16 * 1024 * 1024),
    )(*(pltpu.with_memory_space_constraint(a, pltpu.VMEM) for a in results))


def solution(mesh):
    spec = P(("outer", "inner"), None)
    return jax.shard_map(
        on_device, mesh=mesh, in_specs=(spec, spec, spec), out_specs=spec, check_vma=False
    )
```

```python
import jax
import jax.numpy as jnp
from jax import lax
from jax.experimental import pallas as pl
from jax.experimental.pallas import tpu as pltpu
from jax.sharding import PartitionSpec as P

MESH = pl.DeviceIdType.MESH
F32 = jnp.float32
BF16 = jnp.bfloat16

ROWS = 512
PAIRS = 8
MID = 64
FAR = 2
INNER = 8
RG = 16
GG = 16
BACK = MID + 16
LOWEST = -1e30

INNER_STEPS = ((2, 2), (1, 2), (3, 2), (2, 0), (0, 2), (1, 0), (3, 0))
REST_STEPS = ((2, 1), (2, 3), (1, 1), (1, 3), (3, 1), (3, 3), (0, 1), (0, 3))


def lane_is_second(shape):
    return lax.broadcasted_iota(jnp.int32, shape, len(shape) - 1) >= 64


def split_pair(q):
    second = lane_is_second(q.shape)
    zero = jnp.zeros((), q.dtype)
    return jnp.concatenate([jnp.where(second, zero, q), jnp.where(second, q, zero)], axis=0)


def value_block(v):
    second = lane_is_second(v.shape)
    zero = jnp.zeros((), v.dtype)
    one = jnp.ones((), v.dtype)
    first = jnp.concatenate([jnp.where(second, zero, v), jnp.where(second, zero, one)], axis=1)
    other = jnp.concatenate([jnp.where(second, v, zero), jnp.where(second, one, zero)], axis=1)
    return jnp.concatenate([first, other], axis=0)


def scores_of(q, k):
    return lax.dot_general(split_pair(q), k, (((1,), (1,)), ((), ())), preferred_element_type=F32)


def finish(s, block):
    n = s.shape[0] // 2
    top = jnp.max(s, axis=1, keepdims=True)
    prob = jnp.exp(s - top).astype(BF16)
    both = jnp.concatenate([prob[:n], prob[n:]], axis=1)
    out = jnp.dot(both, block, preferred_element_type=F32)
    total = out[:, 128:]
    second = lane_is_second((n, 128))
    return out[:, :128] / total, jnp.where(second, top[n:], top[:n]) + jnp.log(total)


def parts_of(x):
    high = x.astype(BF16)
    rest = x - high.astype(F32)
    mid = rest.astype(BF16)
    return high, mid, (rest - mid.astype(F32)).astype(BF16)


def pack_lse(lse, groups, width):
    high, mid, low = (p.astype(F32) for p in parts_of(lse))
    lane = lax.broadcasted_iota(jnp.int32, (16, 128), 1) % 64
    out = jnp.zeros((16, 128), F32)
    for g in range(groups):
        rows = slice(16 * g, 16 * g + 16)
        for t, part in enumerate((high, mid, low)):
            out = jnp.where(lane == g * width + t, part[rows], out)
    return out.astype(BF16)


def unpack_lse(packed, groups, width):
    row = lax.broadcasted_iota(jnp.int32, (128, 128), 0)
    lane = lax.broadcasted_iota(jnp.int32, (128, 128), 1)
    out = []
    for g in range(groups):
        at = row % 64 - g * width
        take = jnp.logical_and(jnp.logical_and(at >= 0, at < 3), row // 64 == lane // 64)
        out.append(jnp.dot(packed, jnp.where(take, 1.0, 0.0).astype(BF16), preferred_element_type=F32))
    return out


def kernel(
    q_hbm, k_hbm, v_hbm, merged_ref, two_ref, far_recv,
    q_ref, k_ref, v_ref, edge, load_sem, edge_sem,
    stage, far_stage, mid_send, mid_recv, mid_ssem, mid_rsem,
    back_send, back_recv, back_ssem, back_rsem,
    kv_send, kv_recv, kv_ssem, kv_rsem,
    fq_send, fq_recv, fq_ssem, fq_rsem,
    far_send, far_ssem, far_rsem,
    along_sem, att_ref, lse_pair, lse_ref, far_att, far_lse,
):
    outer = lax.axis_index("outer")
    inner = lax.axis_index("inner")
    core = outer % 2
    z = (outer // 2) % 8
    y_lo = outer // 16
    x = inner // 2
    y_hi = inner % 2

    y = y_hi * 2 + y_lo

    def outer_id(y_lo, z, core):
        return y_lo * 16 + z * 2 + core

    near, along = [], []
    for dx, dy in INNER_STEPS + REST_STEPS:
        px, py = (x + dx) % 4, (y + dy) % 4
        near.append((outer_id(py % 2, z, core), px * 2 + py // 2))
    wave = jnp.minimum(z, 4)
    for pz in range(8):
        for pc in range(2):
            here = jnp.logical_and(z == pz, core == pc)
            later = jnp.where(here, 9, min(pz, 4) - wave)
            along.append(((outer_id(y_lo, pz, pc), inner), later, pz))
    early_along = jnp.where(z < 4, 2 * z + 1, 15)

    entry = sum(9 * v - 2 * (v // 2) - 11 * (v // 3) for v in (x, y))
    opens = jnp.where(entry < 20, 1, 0)
    at_mid = 6 + opens + jnp.where(entry < 5, 1, 0)
    at_far = at_mid
    at_along_early = jnp.where(z < 3, 4 + opens - z, -1)
    at_along_late = jnp.where(z < 4, at_mid - wave + wave // 3, -1)

    barrier = pltpu.get_barrier_semaphore()
    for who in near:
        pl.semaphore_signal(barrier, 1, device_id=who, device_id_type=MESH)
    for who, later, _ in along:
        @pl.when(jnp.logical_and(later >= 0, later < 9))
        def _(who=who):
            pl.semaphore_signal(barrier, 1, device_id=who, device_id_type=MESH)

    edges = []
    for a, src in ((1, k_hbm), (2, v_hbm), (0, q_hbm)):
        for t in range(FAR):
            copy = pltpu.make_async_copy(src.at[pl.ds(256 * t, 16), :], edge.at[a, t], edge_sem.at[a, t])
            copy.start()
            edges.append(copy)
    loads = []
    for a, (src, dst) in enumerate(((q_hbm, q_ref), (k_hbm, k_ref), (v_hbm, v_ref))):
        copy = pltpu.make_async_copy(src, dst, load_sem.at[a])
        copy.start()
        loads.append(copy)

    row16 = lax.broadcasted_iota(jnp.int32, (16, 1024), 0)
    head16 = lax.broadcasted_iota(jnp.int32, (16, 1024), 1) // 64
    my_near = y * 4 + x
    my_along = z * 2 + core

    def pick_edge(a):
        for t in range(FAR):
            block = edge[a, t].astype(F32)
            picked = jnp.sum(jnp.where(row16 == head16, block, 0.0), axis=0, keepdims=True)
            for p in range(PAIRS):
                far_stage[a, pl.ds(2 * p + t, 1), :] = picked[:, 128 * p : 128 * p + 128]

    def kv_copy(who):
        return pltpu.make_async_remote_copy(
            src_ref=kv_send, dst_ref=kv_recv.at[my_along], send_sem=kv_ssem, recv_sem=kv_rsem,
            device_id=who, device_id_type=MESH,
        )

    def fq_copy(who):
        return pltpu.make_async_remote_copy(
            src_ref=fq_send, dst_ref=fq_recv.at[my_near], send_sem=fq_ssem, recv_sem=fq_rsem,
            device_id=who, device_id_type=MESH,
        )

    def mid_copy(who):
        return pltpu.make_async_remote_copy(
            src_ref=mid_send.at[who[1]], dst_ref=mid_recv.at[inner], send_sem=mid_ssem, recv_sem=mid_rsem,
            device_id=who, device_id_type=MESH,
        )

    for copy in edges[:4]:
        copy.wait()
    pick_edge(1)
    pick_edge(2)
    kv_send[0:16, :] = far_stage[1].astype(BF16)
    kv_send[16:32, :] = far_stage[2].astype(BF16)
    kv_recv[my_along] = kv_send[...]
    second = lane_is_second((MID, 128))

    def pick(p):
        first_row = (2 * p) % 8
        columns = pl.ds(pl.multiple_of(p * 128, 128), 128)
        for a, ref in enumerate((q_ref, k_ref, v_ref)):
            wide = ref[:, columns].astype(F32)
            if a == 0:
                wide = wide * 0.125
            stage[a] = wide
        for a in range(3):
            one = stage[a, pl.ds(first_row, MID, stride=8), :]
            two = stage[a, pl.ds(first_row + 1, MID, stride=8), :]
            mid_send[p, pl.ds(MID * a, MID), :] = jnp.where(second, two, one).astype(BF16)


    def pick_all():
        for copy in loads:
            copy.wait()
        for who in near[:7]:
            pick(who[1])

            @pl.when(opens == 0)
            def _(who=who):
                mid_copy(who).start()
        pick(inner)
        mid_recv[inner] = mid_send[inner]

    def meet():
        pl.semaphore_wait(barrier, 15 + early_along)
        for who, later, _ in along:
            @pl.when(later < 0)
            def _(who=who):
                kv_copy(who).start()
        for who, later, _ in along:
            @pl.when(later < 0)
            def _(who=who):
                pl.semaphore_signal(along_sem.at[jnp.where(z < 4, 0, 1)], 1, device_id=who, device_id_type=MESH)
        for who, later, _ in along:
            @pl.when(later == 0)
            def _(who=who):
                kv_copy(who).start()

    def send_mid():
        @pl.when(opens > 0)
        def _():
            for who in near[:7]:
                mid_copy(who).start()

        for copy in edges[4:]:
            copy.wait()
        pick_edge(0)
        fq_send[...] = (far_stage[0] * 0.125).astype(BF16)
        fq_recv[my_near] = fq_send[...]
        for who in near:
            fq_copy(who).start()

    def send_along(half):
        for who, later, pz in along[8 * half : 8 * half + 8]:
            @pl.when(jnp.logical_and(later > 0, later < 9))
            def _(who=who):
                kv_copy(who).start()

    def send_along_early():
        pl.semaphore_wait(along_sem.at[0], 6 - 2 * z)
        send_along(0)

    def send_along_late():
        pl.semaphore_wait(along_sem.at[1], 8)
        send_along(1)

    def middle():
        got = mid_recv.at[pl.ds(0, INNER - 1)]
        pltpu.make_async_copy(got, got, mid_rsem).wait()
        keys = mid_recv[:, MID : 2 * MID, :].reshape(ROWS, 128)
        block = value_block(mid_recv[:, 2 * MID :, :].reshape(ROWS, 128))
        for n in range(4):
            q = mid_recv[2 * n : 2 * n + 2, 0:MID, :].reshape(2 * MID, 128)
            att, lse = finish(scores_of(q, keys), block)
            for s in range(2):
                rows = slice(MID * s, MID * s + MID)
                back_send[2 * n + s, 0:MID, :] = att[rows].astype(BF16)
                back_send[2 * n + s, MID:BACK, :] = pack_lse(lse[rows], 4, 16)
        for who in near[:7]:
            pltpu.make_async_remote_copy(
                src_ref=back_send.at[who[1]], dst_ref=back_recv.at[inner], send_sem=back_ssem, recv_sem=back_rsem,
                device_id=who, device_id_type=MESH,
            ).start()
        back_recv[inner] = back_send[inner]

    def far():
        got = fq_recv.at[pl.ds(0, RG - 1)]
        pltpu.make_async_copy(got, got, fq_rsem).wait()
        stage[1, 0:256, :] = fq_recv[...].reshape(256, 128).astype(F32)
        got = kv_recv.at[pl.ds(0, GG - 1)]
        pltpu.make_async_copy(got, got, kv_rsem).wait()
        stage[0] = kv_recv[...].reshape(ROWS, 128).astype(F32)
        scores, blocks = [], []
        for p in range(PAIRS):
            q = jnp.concatenate([stage[1, pl.ds(2 * p + t, RG, stride=16), :] for t in range(FAR)], axis=0)
            k = jnp.concatenate([stage[0, pl.ds(2 * p + t, GG, stride=32), :] for t in range(FAR)], axis=0)
            v = jnp.concatenate([stage[0, pl.ds(16 + 2 * p + t, GG, stride=32), :] for t in range(FAR)], axis=0)
            scores.append(scores_of(q.astype(BF16), k.astype(BF16)))
            blocks.append(value_block(v.astype(BF16)))
        for p in range(PAIRS):
            att, lse = finish(scores[p], blocks[p])
            for t in range(FAR):
                far_att[pl.ds(2 * p + t, RG, stride=16), :] = att[RG * t : RG * t + RG]
                far_lse[pl.ds(2 * p + t, RG, stride=16), :] = lse[RG * t : RG * t + RG]
        for s in range(RG):
            far_send[s, 0:16, :] = far_att[16 * s : 16 * s + 16, :].astype(BF16)
            far_send[s, 16:32, :] = pack_lse(far_lse[16 * s : 16 * s + 16, :], 1, 16)
        for who in near:
            its_y = who[1] % 2 * 2 + who[0] // 16
            pltpu.make_async_remote_copy(
                src_ref=far_send.at[its_y * 4 + who[1] // 2], dst_ref=far_recv.at[my_near],
                send_sem=far_ssem, recv_sem=far_rsem, device_id=who, device_id_type=MESH,
            ).start()
        far_recv[my_near] = far_send[my_near]

    def first_level(p):
        columns = pl.ds(pl.multiple_of(p * 128, 128), 128)
        keys = k_ref[:, columns]
        block = value_block(v_ref[:, columns])
        for c in range(4):
            rows = pl.ds(128 * c, 128)
            q = q_ref[rows, columns] * jnp.asarray(0.125, BF16)
            att, lse = finish(scores_of(q, keys), block)
            att_ref[p, rows, :] = att
            lse_pair[rows, :] = lse
        first_row = (2 * p) % 8
        one = lse_pair[pl.ds(first_row, MID, stride=8), :]
        two = lse_pair[pl.ds(first_row + 1, MID, stride=8), :]
        lse_ref[p] = jnp.where(second, two, one)

    events = (
        (opens, meet),
        (0, pick_all),
        (opens, send_mid),
        (at_along_early, send_along_early),
        (at_along_late, send_along_late),
        (at_mid, middle),
        (at_far, far),
    )

    def step(t, carry):
        for at, event in events:
            @pl.when(t == at)
            def _(event=event):
                event()

        @pl.when(jnp.logical_and(t > 0, t <= PAIRS))
        def _():
            first_level(t - 1)

        return carry

    lax.fori_loop(0, PAIRS + 2, step, 0)

    got = back_recv.at[pl.ds(0, INNER - 1)]
    pltpu.make_async_copy(got, got, back_rsem).wait()
    mid_lse = unpack_lse(back_recv[:, MID:BACK, :].reshape(128, 128), 4, 16)
    for p in range(PAIRS):
        first_row = (2 * p) % 8
        one = att_ref[p, pl.ds(first_row, MID, stride=8), :]
        two = att_ref[p, pl.ds(first_row + 1, MID, stride=8), :]
        lse1 = lse_ref[p]
        lse2 = jnp.concatenate([mid_lse[g][16 * p : 16 * p + 16] for g in range(4)], axis=0)
        top = jnp.maximum(lse1, lse2)
        w1, w2 = jnp.exp(lse1 - top), jnp.exp(lse2 - top)
        total = w1 + w2
        merged = (w1 * jnp.where(second, two, one) + w2 * back_recv[p, 0:MID, :].astype(F32)) / total
        lse = top + jnp.log(total)
        for t in range(FAR):
            row = 32 * t + p // 4
            two_ref[0, 2 * p + t : 2 * p + t + 1, :] = merged[row : row + 1]
            two_ref[1, 2 * p + t : 2 * p + t + 1, :] = lse[row : row + 1]
        att_ref[p, pl.ds(first_row, MID, stride=8), :] = jnp.where(second, one, merged)
        att_ref[p, pl.ds(first_row + 1, MID, stride=8), :] = jnp.where(second, merged, two)
        merged_ref[:, 128 * p : 128 * p + 128] = att_ref[p].astype(BF16)

    sent = mid_send.at[pl.ds(0, INNER - 1)]
    pltpu.make_async_copy(sent, sent, mid_ssem).wait()
    sent = back_send.at[pl.ds(0, INNER - 1)]
    pltpu.make_async_copy(sent, sent, back_ssem).wait()
    sent = kv_recv.at[pl.ds(0, GG - 1)]
    pltpu.make_async_copy(sent, sent, kv_ssem).wait()
    sent = fq_recv.at[pl.ds(0, RG - 1)]
    pltpu.make_async_copy(sent, sent, fq_ssem).wait()
    sent = far_send.at[pl.ds(0, RG - 1)]
    pltpu.make_async_copy(sent, sent, far_ssem).wait()

    got = far_recv.at[pl.ds(0, RG - 1)]
    pltpu.make_async_copy(got, got, far_rsem).wait()


def merge(merged_ref, two_ref, far_recv, out_hbm, edge, sem):
    copies = []
    for t in range(FAR):
        rest = pl.ds(256 * t + 16, 240)
        copies.append(pltpu.make_async_copy(merged_ref.at[rest, :], out_hbm.at[rest, :], sem.at[t]))
        copies[t].start()

    partial_lse = unpack_lse(far_recv[:, 16:32, :].reshape(256, 128), 1, 16)[0]
    top = two_ref[1]
    for s in range(RG):
        top = jnp.maximum(top, partial_lse[16 * s : 16 * s + 16])
    weight = jnp.exp(two_ref[1] - top)
    numer = weight * two_ref[0]
    denom = weight
    for s in range(RG):
        weight = jnp.exp(partial_lse[16 * s : 16 * s + 16] - top)
        numer = numer + weight * far_recv[s, 0:16, :].astype(F32)
        denom = denom + weight
    result = numer / denom

    row = lax.broadcasted_iota(jnp.int32, (16, 128), 0)
    half = lax.broadcasted_iota(jnp.int32, (16, 128), 1) // 64
    for t in range(FAR):
        for p in range(PAIRS):
            columns = slice(128 * p, 128 * p + 128)
            old = merged_ref[256 * t : 256 * t + 16, columns].astype(F32)
            new = jnp.where(row == 2 * p + half, result[2 * p + t : 2 * p + t + 1], old)
            edge[t, :, columns] = new.astype(BF16)
        copies.append(pltpu.make_async_copy(edge.at[t], out_hbm.at[pl.ds(256 * t, 16), :], sem.at[FAR + t]))
        copies[FAR + t].start()
    for copy in copies:
        copy.wait()


def on_device(queries, keys, values):
    dma = pltpu.SemaphoreType.DMA
    vmem = pltpu.VMEM
    results = pl.pallas_call(
        kernel,
        out_shape=[
            vmem((ROWS, 1024), BF16), vmem((2, 16, 128), F32), vmem((RG, 32, 128), BF16),
        ],
        in_specs=[pl.BlockSpec(memory_space=pltpu.HBM)] * 3,
        out_specs=[pl.BlockSpec(memory_space=pltpu.VMEM)] * 3,
        scratch_shapes=[
            vmem((ROWS, 1024), BF16), vmem((ROWS, 1024), BF16), vmem((ROWS, 1024), BF16),
            vmem((3, FAR, 16, 1024), BF16), dma((3,)), dma((3, FAR)),
            vmem((3, ROWS, 128), F32), vmem((3, 16, 128), F32),
            vmem((INNER, 3 * MID, 128), BF16), vmem((INNER, 3 * MID, 128), BF16), dma, dma,
            vmem((INNER, BACK, 128), BF16), vmem((INNER, BACK, 128), BF16), dma, dma,
            vmem((32, 128), BF16), vmem((GG, 32, 128), BF16), dma, dma,
            vmem((16, 128), BF16), vmem((RG, 16, 128), BF16), dma, dma,
            vmem((RG, 32, 128), BF16), dma, dma,
            pltpu.SemaphoreType.REGULAR((2,)),
            vmem((PAIRS, ROWS, 128), F32), vmem((ROWS, 128), F32), vmem((PAIRS, MID, 128), F32),
            vmem((256, 128), F32), vmem((256, 128), F32),
        ],
        compiler_params=pltpu.CompilerParams(
            collective_id=0, has_side_effects=True, vmem_limit_bytes=40 * 1024 * 1024
        ),
    )(*(pltpu.with_memory_space_constraint(a, pltpu.HBM) for a in (queries, keys, values)))
    return pl.pallas_call(
        merge,
        out_shape=pltpu.HBM((ROWS, 1024), BF16),
        in_specs=[pl.BlockSpec(memory_space=pltpu.VMEM)] * 3,
        out_specs=pl.BlockSpec(memory_space=pltpu.HBM),
        scratch_shapes=[
            vmem((FAR, 16, 1024), BF16), dma((2 * FAR,)),
        ],
        compiler_params=pltpu.CompilerParams(vmem_limit_bytes=16 * 1024 * 1024),
    )(*(pltpu.with_memory_space_constraint(a, pltpu.VMEM) for a in results))


def solution(mesh):
    spec = P(("outer", "inner"), None)
    return jax.shard_map(
        on_device, mesh=mesh, in_specs=(spec, spec, spec), out_specs=spec, check_vma=False
    )
```

```python
import jax
import jax.numpy as jnp
from jax import lax
from jax.experimental import pallas as pl
from jax.experimental.pallas import tpu as pltpu
from jax.sharding import PartitionSpec as P

MESH = pl.DeviceIdType.MESH
F32 = jnp.float32
BF16 = jnp.bfloat16

ROWS = 512
PAIRS = 8
MID = 64
FAR = 2
INNER = 8
RG = 16
GG = 16
LOWEST = -1e30

INNER_STEPS = ((2, 2), (1, 2), (3, 2), (2, 0), (0, 2), (1, 0), (3, 0))
REST_STEPS = ((2, 1), (2, 3), (1, 1), (1, 3), (3, 1), (3, 3), (0, 1), (0, 3))


def lane_is_second(shape):
    return lax.broadcasted_iota(jnp.int32, shape, len(shape) - 1) >= 64


def split_pair(q):
    second = lane_is_second(q.shape)
    zero = jnp.zeros((), q.dtype)
    return jnp.concatenate([jnp.where(second, zero, q), jnp.where(second, q, zero)], axis=0)


def value_block(v):
    second = lane_is_second(v.shape)
    zero = jnp.zeros((), v.dtype)
    one = jnp.ones((), v.dtype)
    first = jnp.concatenate([jnp.where(second, zero, v), jnp.where(second, zero, one)], axis=1)
    other = jnp.concatenate([jnp.where(second, v, zero), jnp.where(second, one, zero)], axis=1)
    return jnp.concatenate([first, other], axis=0)


def scores_of(q, k):
    return lax.dot_general(split_pair(q), k, (((1,), (1,)), ((), ())), preferred_element_type=F32)


def finish(s, block):
    n = s.shape[0] // 2
    top = jnp.max(s, axis=1, keepdims=True)
    prob = jnp.exp(s - top).astype(BF16)
    both = jnp.concatenate([prob[:n], prob[n:]], axis=1)
    out = jnp.dot(both, block, preferred_element_type=F32)
    total = out[:, 128:]
    second = lane_is_second((n, 128))
    return out[:, :128] / total, jnp.where(second, top[n:], top[:n]) + jnp.log(total)


def parts_of(x):
    high = x.astype(BF16)
    rest = x - high.astype(F32)
    mid = rest.astype(BF16)
    return high, mid, (rest - mid.astype(F32)).astype(BF16)


def diagonal(rows, parts, width):
    row = lax.broadcasted_iota(jnp.int32, (rows, 128), 0)
    lane = lax.broadcasted_iota(jnp.int32, (rows, 128), 1) % 64
    return [lane == row + t * width for t in range(parts)]


def lse_rows(lse, wide):
    n = lse.shape[0]
    masks = diagonal(n, 3, 0 if wide else 16)
    picked = [
        jnp.sum(jnp.where(mask, part.astype(F32), 0.0), axis=0, keepdims=True)
        for mask, part in zip(masks, parts_of(lse), strict=True)
    ]
    return jnp.concatenate(picked, axis=1) if wide else picked[0] + picked[1] + picked[2]


def half_sums(width):
    row = lax.broadcasted_iota(jnp.int32, (width, 128), 0)
    lane = lax.broadcasted_iota(jnp.int32, (width, 128), 1)
    return jnp.where(row % 128 // 64 == lane // 64, 1.0, 0.0).astype(BF16)


def kernel(
    q_hbm, k_hbm, v_hbm, merged_ref, two_ref, far_recv, far_lse_recv,
    q_ref, k_ref, v_ref, edge, load_sem, edge_sem,
    stage, far_stage, mid_send, mid_recv, mid_ssem, mid_rsem,
    back_send, back_recv, back_ssem, back_rsem, back_lse_send, back_lse_recv, far_lse_send, lse_ssem, lse_rsem,
    kv_send, kv_recv, kv_ssem, kv_rsem,
    fq_send, fq_recv, fq_ssem, fq_rsem,
    far_send, far_ssem, far_rsem,
    along_sem, att_ref, lse_pair, lse_ref, far_att, far_lse,
):
    outer = lax.axis_index("outer")
    inner = lax.axis_index("inner")
    core = outer % 2
    z = (outer // 2) % 8
    y_lo = outer // 16
    x = inner // 2
    y_hi = inner % 2

    y = y_hi * 2 + y_lo

    def outer_id(y_lo, z, core):
        return y_lo * 16 + z * 2 + core

    near, along = [], []
    for dx, dy in INNER_STEPS + REST_STEPS:
        px, py = (x + dx) % 4, (y + dy) % 4
        near.append((outer_id(py % 2, z, core), px * 2 + py // 2))
    wave = jnp.minimum(z, 4)
    for pz in range(8):
        for pc in range(2):
            here = jnp.logical_and(z == pz, core == pc)
            later = jnp.where(here, 9, min(pz, 4) - wave)
            along.append(((outer_id(y_lo, pz, pc), inner), later, pz))
    early_along = jnp.where(z < 4, 2 * z + 1, 15)

    entry = sum(9 * v - 2 * (v // 2) - 11 * (v // 3) for v in (x, y))
    opens = jnp.where(entry < 20, 1, 0)
    at_mid = 6 + opens + jnp.where(entry < 5, 1, 0)
    at_far = at_mid
    at_along_early = jnp.where(z < 3, 4 + opens - z, -1)
    at_along_late = jnp.where(z < 4, at_mid - wave + wave // 3, -1)

    barrier = pltpu.get_barrier_semaphore()
    for who in near:
        pl.semaphore_signal(barrier, 1, device_id=who, device_id_type=MESH)
    for who, later, _ in along:
        @pl.when(jnp.logical_and(later >= 0, later < 9))
        def _(who=who):
            pl.semaphore_signal(barrier, 1, device_id=who, device_id_type=MESH)

    edges = []
    for a, src in ((1, k_hbm), (2, v_hbm), (0, q_hbm)):
        for t in range(FAR):
            copy = pltpu.make_async_copy(src.at[pl.ds(256 * t, 16), :], edge.at[a, t], edge_sem.at[a, t])
            copy.start()
            edges.append(copy)
    loads = []
    for a, (src, dst) in enumerate(((q_hbm, q_ref), (k_hbm, k_ref), (v_hbm, v_ref))):
        copy = pltpu.make_async_copy(src, dst, load_sem.at[a])
        copy.start()
        loads.append(copy)

    row16 = lax.broadcasted_iota(jnp.int32, (16, 1024), 0)
    head16 = lax.broadcasted_iota(jnp.int32, (16, 1024), 1) // 64
    my_near = y * 4 + x
    my_along = z * 2 + core

    def pick_edge(a):
        for t in range(FAR):
            block = edge[a, t].astype(F32)
            picked = jnp.sum(jnp.where(row16 == head16, block, 0.0), axis=0, keepdims=True)
            for p in range(PAIRS):
                far_stage[a, pl.ds(2 * p + t, 1), :] = picked[:, 128 * p : 128 * p + 128]

    def kv_copy(who):
        return pltpu.make_async_remote_copy(
            src_ref=kv_send, dst_ref=kv_recv.at[my_along], send_sem=kv_ssem, recv_sem=kv_rsem,
            device_id=who, device_id_type=MESH,
        )

    def fq_copy(who):
        return pltpu.make_async_remote_copy(
            src_ref=fq_send, dst_ref=fq_recv.at[my_near], send_sem=fq_ssem, recv_sem=fq_rsem,
            device_id=who, device_id_type=MESH,
        )

    def mid_copy(who):
        return pltpu.make_async_remote_copy(
            src_ref=mid_send.at[who[1]], dst_ref=mid_recv.at[inner], send_sem=mid_ssem, recv_sem=mid_rsem,
            device_id=who, device_id_type=MESH,
        )

    for copy in edges[:4]:
        copy.wait()
    pick_edge(1)
    pick_edge(2)
    kv_send[0:16, :] = far_stage[1].astype(BF16)
    kv_send[16:32, :] = far_stage[2].astype(BF16)
    kv_recv[my_along] = kv_send[...]
    second = lane_is_second((MID, 128))

    def pick(p):
        first_row = (2 * p) % 8
        columns = pl.ds(pl.multiple_of(p * 128, 128), 128)
        for a, ref in enumerate((q_ref, k_ref, v_ref)):
            wide = ref[:, columns].astype(F32)
            if a == 0:
                wide = wide * 0.125
            stage[a] = wide
        for a in range(3):
            one = stage[a, pl.ds(first_row, MID, stride=8), :]
            two = stage[a, pl.ds(first_row + 1, MID, stride=8), :]
            mid_send[p, pl.ds(MID * a, MID), :] = jnp.where(second, two, one).astype(BF16)


    def pick_all():
        for copy in loads:
            copy.wait()
        for who in near[:7]:
            pick(who[1])

            @pl.when(opens == 0)
            def _(who=who):
                mid_copy(who).start()
        pick(inner)
        mid_recv[inner] = mid_send[inner]

    def meet():
        pl.semaphore_wait(barrier, 15 + early_along)
        for who, later, _ in along:
            @pl.when(later < 0)
            def _(who=who):
                kv_copy(who).start()
        for who, later, _ in along:
            @pl.when(later < 0)
            def _(who=who):
                pl.semaphore_signal(along_sem.at[jnp.where(z < 4, 0, 1)], 1, device_id=who, device_id_type=MESH)
        for who, later, _ in along:
            @pl.when(later == 0)
            def _(who=who):
                kv_copy(who).start()

    def send_mid():
        @pl.when(opens > 0)
        def _():
            for who in near[:7]:
                mid_copy(who).start()

        for copy in edges[4:]:
            copy.wait()
        pick_edge(0)
        fq_send[...] = (far_stage[0] * 0.125).astype(BF16)
        fq_recv[my_near] = fq_send[...]
        for who in near:
            fq_copy(who).start()

    def send_along(half):
        for who, later, pz in along[8 * half : 8 * half + 8]:
            @pl.when(jnp.logical_and(later > 0, later < 9))
            def _(who=who):
                kv_copy(who).start()

    def send_along_early():
        pl.semaphore_wait(along_sem.at[0], 6 - 2 * z)
        send_along(0)

    def send_along_late():
        pl.semaphore_wait(along_sem.at[1], 8)
        send_along(1)

    def middle():
        got = mid_recv.at[pl.ds(0, INNER - 1)]
        pltpu.make_async_copy(got, got, mid_rsem).wait()
        keys = mid_recv[:, MID : 2 * MID, :].reshape(ROWS, 128)
        block = value_block(mid_recv[:, 2 * MID :, :].reshape(ROWS, 128))
        for n in range(4):
            q = mid_recv[2 * n : 2 * n + 2, 0:MID, :].reshape(2 * MID, 128)
            att, lse = finish(scores_of(q, keys), block)
            for s in range(2):
                rows = slice(MID * s, MID * s + MID)
                back_send[2 * n + s] = att[rows].astype(BF16)
                back_lse_send[2 * n + s] = lse_rows(lse[rows], True)
        for who in near[:7]:
            pltpu.make_async_remote_copy(
                src_ref=back_send.at[who[1]], dst_ref=back_recv.at[inner], send_sem=back_ssem, recv_sem=back_rsem,
                device_id=who, device_id_type=MESH,
            ).start()
            pltpu.make_async_remote_copy(
                src_ref=back_lse_send.at[who[1]], dst_ref=back_lse_recv.at[inner],
                send_sem=lse_ssem.at[0], recv_sem=lse_rsem.at[0], device_id=who, device_id_type=MESH,
            ).start()
        back_recv[inner] = back_send[inner]
        back_lse_recv[inner] = back_lse_send[inner]

    def far():
        got = fq_recv.at[pl.ds(0, RG - 1)]
        pltpu.make_async_copy(got, got, fq_rsem).wait()
        stage[1, 0:256, :] = fq_recv[...].reshape(256, 128).astype(F32)
        got = kv_recv.at[pl.ds(0, GG - 1)]
        pltpu.make_async_copy(got, got, kv_rsem).wait()
        stage[0] = kv_recv[...].reshape(ROWS, 128).astype(F32)
        scores, blocks = [], []
        for p in range(PAIRS):
            q = jnp.concatenate([stage[1, pl.ds(2 * p + t, RG, stride=16), :] for t in range(FAR)], axis=0)
            k = jnp.concatenate([stage[0, pl.ds(2 * p + t, GG, stride=32), :] for t in range(FAR)], axis=0)
            v = jnp.concatenate([stage[0, pl.ds(16 + 2 * p + t, GG, stride=32), :] for t in range(FAR)], axis=0)
            scores.append(scores_of(q.astype(BF16), k.astype(BF16)))
            blocks.append(value_block(v.astype(BF16)))
        for p in range(PAIRS):
            att, lse = finish(scores[p], blocks[p])
            for t in range(FAR):
                far_att[pl.ds(2 * p + t, RG, stride=16), :] = att[RG * t : RG * t + RG]
                far_lse[pl.ds(2 * p + t, RG, stride=16), :] = lse[RG * t : RG * t + RG]
        for s in range(RG):
            far_send[s] = far_att[16 * s : 16 * s + 16, :].astype(BF16)
            far_lse_send[s] = lse_rows(far_lse[16 * s : 16 * s + 16, :], False)
        for who in near:
            its_y = who[1] % 2 * 2 + who[0] // 16
            pltpu.make_async_remote_copy(
                src_ref=far_send.at[its_y * 4 + who[1] // 2], dst_ref=far_recv.at[my_near],
                send_sem=far_ssem, recv_sem=far_rsem, device_id=who, device_id_type=MESH,
            ).start()
            pltpu.make_async_remote_copy(
                src_ref=far_lse_send.at[its_y * 4 + who[1] // 2], dst_ref=far_lse_recv.at[my_near],
                send_sem=lse_ssem.at[1], recv_sem=lse_rsem.at[1], device_id=who, device_id_type=MESH,
            ).start()
        far_recv[my_near] = far_send[my_near]
        far_lse_recv[my_near] = far_lse_send[my_near]

    def first_level(p):
        columns = pl.ds(pl.multiple_of(p * 128, 128), 128)
        keys = k_ref[:, columns]
        block = value_block(v_ref[:, columns])
        for c in range(4):
            rows = pl.ds(128 * c, 128)
            q = q_ref[rows, columns] * jnp.asarray(0.125, BF16)
            att, lse = finish(scores_of(q, keys), block)
            att_ref[p, rows, :] = att
            lse_pair[rows, :] = lse
        first_row = (2 * p) % 8
        one = lse_pair[pl.ds(first_row, MID, stride=8), :]
        two = lse_pair[pl.ds(first_row + 1, MID, stride=8), :]
        lse_ref[p] = jnp.where(second, two, one)

    events = (
        (opens, meet),
        (0, pick_all),
        (opens, send_mid),
        (at_along_early, send_along_early),
        (at_along_late, send_along_late),
        (at_mid, middle),
        (at_far, far),
    )

    def step(t, carry):
        for at, event in events:
            @pl.when(t == at)
            def _(event=event):
                event()

        @pl.when(jnp.logical_and(t > 0, t <= PAIRS))
        def _():
            first_level(t - 1)

        return carry

    lax.fori_loop(0, PAIRS + 2, step, 0)

    got = back_recv.at[pl.ds(0, INNER - 1)]
    pltpu.make_async_copy(got, got, back_rsem).wait()
    got = back_lse_recv.at[pl.ds(0, INNER - 1)]
    pltpu.make_async_copy(got, got, lse_rsem.at[0]).wait()
    mask = jnp.concatenate(diagonal(MID, 3, 0), axis=1)
    spread = half_sums(3 * 128)
    for p in range(PAIRS):
        first_row = (2 * p) % 8
        one = att_ref[p, pl.ds(first_row, MID, stride=8), :]
        two = att_ref[p, pl.ds(first_row + 1, MID, stride=8), :]
        lse1 = lse_ref[p]
        lse2 = jnp.where(mask, back_lse_recv[p], 0.0).astype(BF16)
        lse2 = jnp.dot(lse2, spread, preferred_element_type=F32)
        top = jnp.maximum(lse1, lse2)
        w1, w2 = jnp.exp(lse1 - top), jnp.exp(lse2 - top)
        total = w1 + w2
        merged = (w1 * jnp.where(second, two, one) + w2 * back_recv[p].astype(F32)) / total
        lse = top + jnp.log(total)
        for t in range(FAR):
            row = 32 * t + p // 4
            two_ref[0, 2 * p + t : 2 * p + t + 1, :] = merged[row : row + 1]
            two_ref[1, 2 * p + t : 2 * p + t + 1, :] = lse[row : row + 1]
        att_ref[p, pl.ds(first_row, MID, stride=8), :] = jnp.where(second, one, merged)
        att_ref[p, pl.ds(first_row + 1, MID, stride=8), :] = jnp.where(second, merged, two)
        merged_ref[:, 128 * p : 128 * p + 128] = att_ref[p].astype(BF16)

    sent = mid_send.at[pl.ds(0, INNER - 1)]
    pltpu.make_async_copy(sent, sent, mid_ssem).wait()
    sent = back_send.at[pl.ds(0, INNER - 1)]
    pltpu.make_async_copy(sent, sent, back_ssem).wait()
    sent = kv_recv.at[pl.ds(0, GG - 1)]
    pltpu.make_async_copy(sent, sent, kv_ssem).wait()
    sent = fq_recv.at[pl.ds(0, RG - 1)]
    pltpu.make_async_copy(sent, sent, fq_ssem).wait()
    sent = far_send.at[pl.ds(0, RG - 1)]
    pltpu.make_async_copy(sent, sent, far_ssem).wait()
    sent = back_lse_send.at[pl.ds(0, INNER - 1)]
    pltpu.make_async_copy(sent, sent, lse_ssem.at[0]).wait()
    sent = far_lse_send.at[pl.ds(0, RG - 1)]
    pltpu.make_async_copy(sent, sent, lse_ssem.at[1]).wait()

    got = far_recv.at[pl.ds(0, RG - 1)]
    pltpu.make_async_copy(got, got, far_rsem).wait()
    got = far_lse_recv.at[pl.ds(0, RG - 1)]
    pltpu.make_async_copy(got, got, lse_rsem.at[1]).wait()


def merge(merged_ref, two_ref, far_recv, far_lse_recv, out_hbm, edge, sem):
    copies = []
    for t in range(FAR):
        rest = pl.ds(256 * t + 16, 240)
        copies.append(pltpu.make_async_copy(merged_ref.at[rest, :], out_hbm.at[rest, :], sem.at[t]))
        copies[t].start()

    mask = diagonal(16, 3, 16)
    mask = jnp.logical_or(jnp.logical_or(mask[0], mask[1]), mask[2])
    partial_lse = jnp.concatenate([jnp.where(mask, far_lse_recv[s], 0.0) for s in range(RG)], axis=0).astype(BF16)
    partial_lse = jnp.dot(partial_lse, half_sums(128), preferred_element_type=F32)
    top = two_ref[1]
    for s in range(RG):
        top = jnp.maximum(top, partial_lse[16 * s : 16 * s + 16])
    weight = jnp.exp(two_ref[1] - top)
    numer = weight * two_ref[0]
    denom = weight
    for s in range(RG):
        weight = jnp.exp(partial_lse[16 * s : 16 * s + 16] - top)
        numer = numer + weight * far_recv[s].astype(F32)
        denom = denom + weight
    result = numer / denom

    row = lax.broadcasted_iota(jnp.int32, (16, 128), 0)
    half = lax.broadcasted_iota(jnp.int32, (16, 128), 1) // 64
    for t in range(FAR):
        for p in range(PAIRS):
            columns = slice(128 * p, 128 * p + 128)
            old = merged_ref[256 * t : 256 * t + 16, columns].astype(F32)
            new = jnp.where(row == 2 * p + half, result[2 * p + t : 2 * p + t + 1], old)
            edge[t, :, columns] = new.astype(BF16)
        copies.append(pltpu.make_async_copy(edge.at[t], out_hbm.at[pl.ds(256 * t, 16), :], sem.at[FAR + t]))
        copies[FAR + t].start()
    for copy in copies:
        copy.wait()


def on_device(queries, keys, values):
    dma = pltpu.SemaphoreType.DMA
    vmem = pltpu.VMEM
    results = pl.pallas_call(
        kernel,
        out_shape=[
            vmem((ROWS, 1024), BF16), vmem((2, 16, 128), F32), vmem((RG, 16, 128), BF16), vmem((RG, 1, 128), F32),
        ],
        in_specs=[pl.BlockSpec(memory_space=pltpu.HBM)] * 3,
        out_specs=[pl.BlockSpec(memory_space=pltpu.VMEM)] * 4,
        scratch_shapes=[
            vmem((ROWS, 1024), BF16), vmem((ROWS, 1024), BF16), vmem((ROWS, 1024), BF16),
            vmem((3, FAR, 16, 1024), BF16), dma((3,)), dma((3, FAR)),
            vmem((3, ROWS, 128), F32), vmem((3, 16, 128), F32),
            vmem((INNER, 3 * MID, 128), BF16), vmem((INNER, 3 * MID, 128), BF16), dma, dma,
            vmem((INNER, MID, 128), BF16), vmem((INNER, MID, 128), BF16), dma, dma,
            vmem((INNER, 1, 384), F32), vmem((INNER, 1, 384), F32), vmem((RG, 1, 128), F32), dma((2,)), dma((2,)),
            vmem((32, 128), BF16), vmem((GG, 32, 128), BF16), dma, dma,
            vmem((16, 128), BF16), vmem((RG, 16, 128), BF16), dma, dma,
            vmem((RG, 16, 128), BF16), dma, dma,
            pltpu.SemaphoreType.REGULAR((2,)),
            vmem((PAIRS, ROWS, 128), F32), vmem((ROWS, 128), F32), vmem((PAIRS, MID, 128), F32),
            vmem((256, 128), F32), vmem((256, 128), F32),
        ],
        compiler_params=pltpu.CompilerParams(
            collective_id=0, has_side_effects=True, vmem_limit_bytes=40 * 1024 * 1024
        ),
    )(*(pltpu.with_memory_space_constraint(a, pltpu.HBM) for a in (queries, keys, values)))
    return pl.pallas_call(
        merge,
        out_shape=pltpu.HBM((ROWS, 1024), BF16),
        in_specs=[pl.BlockSpec(memory_space=pltpu.VMEM)] * 4,
        out_specs=pl.BlockSpec(memory_space=pltpu.HBM),
        scratch_shapes=[
            vmem((FAR, 16, 1024), BF16), dma((2 * FAR,)),
        ],
        compiler_params=pltpu.CompilerParams(vmem_limit_bytes=16 * 1024 * 1024),
    )(*(pltpu.with_memory_space_constraint(a, pltpu.VMEM) for a in results))


def solution(mesh):
    spec = P(("outer", "inner"), None)
    return jax.shard_map(
        on_device, mesh=mesh, in_specs=(spec, spec, spec), out_specs=spec, check_vma=False
    )
```

```python
import jax
import jax.numpy as jnp
from jax import lax
from jax.experimental import pallas as pl
from jax.experimental.pallas import tpu as pltpu
from jax.sharding import PartitionSpec as P

MESH = pl.DeviceIdType.MESH
F32 = jnp.float32
BF16 = jnp.bfloat16

ROWS = 512
PAIRS = 8
MID = 64
FAR = 2
INNER = 8
RG = 16
GG = 16
LOWEST = -1e30

INNER_STEPS = ((2, 2), (1, 2), (3, 2), (2, 0), (0, 2), (1, 0), (3, 0))
REST_STEPS = ((2, 1), (2, 3), (1, 1), (1, 3), (3, 1), (3, 3), (0, 1), (0, 3))


def lane_is_second(shape):
    return lax.broadcasted_iota(jnp.int32, shape, len(shape) - 1) >= 64


def split_pair(q):
    second = lane_is_second(q.shape)
    zero = jnp.zeros((), q.dtype)
    return jnp.concatenate([jnp.where(second, zero, q), jnp.where(second, q, zero)], axis=0)


def value_block(v):
    second = lane_is_second(v.shape)
    zero = jnp.zeros((), v.dtype)
    one = jnp.ones((), v.dtype)
    first = jnp.concatenate([jnp.where(second, zero, v), jnp.where(second, zero, one)], axis=1)
    other = jnp.concatenate([jnp.where(second, v, zero), jnp.where(second, one, zero)], axis=1)
    return jnp.concatenate([first, other], axis=0)


def scores_of(q, k):
    return lax.dot_general(split_pair(q), k, (((1,), (1,)), ((), ())), preferred_element_type=F32)


def finish(s, block):
    n = s.shape[0] // 2
    top = jnp.max(s, axis=1, keepdims=True)
    prob = jnp.exp(s - top).astype(BF16)
    both = jnp.concatenate([prob[:n], prob[n:]], axis=1)
    out = jnp.dot(both, block, preferred_element_type=F32)
    total = out[:, 128:]
    second = lane_is_second((n, 128))
    return out[:, :128] / total, jnp.where(second, top[n:], top[:n]) + jnp.log(total)


def parts_of(x):
    high = x.astype(BF16)
    rest = x - high.astype(F32)
    mid = rest.astype(BF16)
    return high, mid, (rest - mid.astype(F32)).astype(BF16)


def diagonal(rows, parts, width):
    row = lax.broadcasted_iota(jnp.int32, (rows, 128), 0)
    lane = lax.broadcasted_iota(jnp.int32, (rows, 128), 1) % 64
    return [lane == row + t * width for t in range(parts)]


def lse_rows(lse, wide):
    n = lse.shape[0]
    masks = diagonal(n, 3, 0 if wide else 16)
    picked = [
        jnp.sum(jnp.where(mask, part.astype(F32), 0.0), axis=0, keepdims=True)
        for mask, part in zip(masks, parts_of(lse), strict=True)
    ]
    return jnp.concatenate(picked, axis=1) if wide else picked[0] + picked[1] + picked[2]


def half_sums(width):
    row = lax.broadcasted_iota(jnp.int32, (width, 128), 0)
    lane = lax.broadcasted_iota(jnp.int32, (width, 128), 1)
    return jnp.where(row % 128 // 64 == lane // 64, 1.0, 0.0).astype(BF16)


def kernel(
    q_hbm, k_hbm, v_hbm, merged_ref, two_ref, far_recv, far_lse_recv,
    q_ref, k_ref, v_ref, edge, load_sem, edge_sem,
    stage, far_stage, mid_send, mid_recv, mid_ssem, mid_rsem,
    back_send, back_recv, back_ssem, back_rsem, back_lse_send, back_lse_recv, far_lse_send, lse_ssem, lse_rsem,
    kv_send, kv_recv, kv_ssem, kv_rsem,
    fq_send, fq_recv, fq_ssem, fq_rsem,
    far_send, far_ssem, far_rsem,
    along_sem, att_ref, lse_pair, lse_ref, far_att, far_lse,
):
    outer = lax.axis_index("outer")
    inner = lax.axis_index("inner")
    core = outer % 2
    z = (outer // 2) % 8
    y_lo = outer // 16
    x = inner // 2
    y_hi = inner % 2

    y = y_hi * 2 + y_lo

    def outer_id(y_lo, z, core):
        return y_lo * 16 + z * 2 + core

    near, along = [], []
    for dx, dy in INNER_STEPS + REST_STEPS:
        px, py = (x + dx) % 4, (y + dy) % 4
        near.append((outer_id(py % 2, z, core), px * 2 + py // 2))
    wave = jnp.minimum(z, 4)
    for pz in range(8):
        for pc in range(2):
            here = jnp.logical_and(z == pz, core == pc)
            later = jnp.where(here, 9, min(pz, 4) - wave)
            along.append(((outer_id(y_lo, pz, pc), inner), later, pz))
    early_along = jnp.where(z < 4, 2 * z + 1, 15)

    entry = sum(9 * v - 2 * (v // 2) - 11 * (v // 3) for v in (x, y))
    opens = jnp.where(entry < 20, 1, 0)
    at_mid = 6 + opens + jnp.where(entry < 5, 1, 0)
    at_far = at_mid
    at_along_early = jnp.where(z < 3, 4 + opens - z, -1)
    at_along_late = jnp.where(z < 4, at_mid - wave + wave // 3, -1)

    barrier = pltpu.get_barrier_semaphore()
    def speak_along(peers):
        for who, later, _ in peers:
            @pl.when(jnp.logical_and(later >= 0, later < 9))
            def _(who=who):
                pl.semaphore_signal(barrier, 1, device_id=who, device_id_type=MESH)

    @pl.when(z >= 4)
    def _():
        speak_along(along[8:])

    for who in near:
        pl.semaphore_signal(barrier, 1, device_id=who, device_id_type=MESH)

    @pl.when(z < 4)
    def _():
        speak_along(along)

    edges = []
    for a, src in ((1, k_hbm), (2, v_hbm), (0, q_hbm)):
        for t in range(FAR):
            copy = pltpu.make_async_copy(src.at[pl.ds(256 * t, 16), :], edge.at[a, t], edge_sem.at[a, t])
            copy.start()
            edges.append(copy)
    loads = []
    for a, (src, dst) in enumerate(((q_hbm, q_ref), (k_hbm, k_ref), (v_hbm, v_ref))):
        copy = pltpu.make_async_copy(src, dst, load_sem.at[a])
        copy.start()
        loads.append(copy)

    row16 = lax.broadcasted_iota(jnp.int32, (16, 1024), 0)
    head16 = lax.broadcasted_iota(jnp.int32, (16, 1024), 1) // 64
    my_near = y * 4 + x
    my_along = z * 2 + core

    def pick_edge(a):
        for t in range(FAR):
            block = edge[a, t].astype(F32)
            picked = jnp.sum(jnp.where(row16 == head16, block, 0.0), axis=0, keepdims=True)
            for p in range(PAIRS):
                far_stage[a, pl.ds(2 * p + t, 1), :] = picked[:, 128 * p : 128 * p + 128]

    def kv_copy(who):
        return pltpu.make_async_remote_copy(
            src_ref=kv_send, dst_ref=kv_recv.at[my_along], send_sem=kv_ssem, recv_sem=kv_rsem,
            device_id=who, device_id_type=MESH,
        )

    def fq_copy(who):
        return pltpu.make_async_remote_copy(
            src_ref=fq_send, dst_ref=fq_recv.at[my_near], send_sem=fq_ssem, recv_sem=fq_rsem,
            device_id=who, device_id_type=MESH,
        )

    def mid_copy(who):
        return pltpu.make_async_remote_copy(
            src_ref=mid_send.at[who[1]], dst_ref=mid_recv.at[inner], send_sem=mid_ssem, recv_sem=mid_rsem,
            device_id=who, device_id_type=MESH,
        )

    for copy in edges[:4]:
        copy.wait()
    pick_edge(1)
    pick_edge(2)
    kv_send[0:16, :] = far_stage[1].astype(BF16)
    kv_send[16:32, :] = far_stage[2].astype(BF16)
    kv_recv[my_along] = kv_send[...]
    second = lane_is_second((MID, 128))

    def pick(p):
        first_row = (2 * p) % 8
        columns = pl.ds(pl.multiple_of(p * 128, 128), 128)
        for a, ref in enumerate((q_ref, k_ref, v_ref)):
            wide = ref[:, columns].astype(F32)
            if a == 0:
                wide = wide * 0.125
            stage[a, 0:ROWS, :] = wide
        for a in range(3):
            one = stage[a, pl.ds(first_row, MID, stride=8), :]
            two = stage[a, pl.ds(first_row + 1, MID, stride=8), :]
            mid_send[p, pl.ds(MID * a, MID), :] = jnp.where(second, two, one).astype(BF16)


    def pick_all():
        for copy in loads:
            copy.wait()
        for who in near[:7]:
            pick(who[1])

            @pl.when(opens == 0)
            def _(who=who):
                mid_copy(who).start()
        pick(inner)
        mid_recv[inner] = mid_send[inner]

    def meet():
        pl.semaphore_wait(barrier, 15 + early_along)
        for who, later, _ in along:
            @pl.when(later < 0)
            def _(who=who):
                kv_copy(who).start()
        for who, later, _ in along:
            @pl.when(later < 0)
            def _(who=who):
                pl.semaphore_signal(along_sem.at[jnp.where(z < 4, 0, 1)], 1, device_id=who, device_id_type=MESH)
        for who, later, _ in along:
            @pl.when(later == 0)
            def _(who=who):
                kv_copy(who).start()

    def send_mid():
        for copy in edges[4:]:
            copy.wait()
        pick_edge(0)
        fq_send[...] = (far_stage[0] * 0.125).astype(BF16)
        fq_recv[my_near] = fq_send[...]
        distant = near[:3] + near[7:9]
        for who in distant:
            fq_copy(who).start()

        @pl.when(opens > 0)
        def _():
            for who in near[:7]:
                mid_copy(who).start()

        for who in near[3:7] + near[9:]:
            fq_copy(who).start()

    def send_along(half):
        for who, later, pz in along[8 * half : 8 * half + 8]:
            @pl.when(jnp.logical_and(later > 0, later < 9))
            def _(who=who):
                kv_copy(who).start()

    def send_along_early():
        pl.semaphore_wait(along_sem.at[0], 6 - 2 * z)
        send_along(0)

    def send_along_late():
        pl.semaphore_wait(along_sem.at[1], 8)
        send_along(1)

    def middle():
        got = mid_recv.at[pl.ds(0, INNER - 1)]
        pltpu.make_async_copy(got, got, mid_rsem).wait()
        keys = mid_recv[:, MID : 2 * MID, :].reshape(ROWS, 128)
        block = value_block(mid_recv[:, 2 * MID :, :].reshape(ROWS, 128))
        for n in range(4):
            q = mid_recv[2 * n : 2 * n + 2, 0:MID, :].reshape(2 * MID, 128)
            att, lse = finish(scores_of(q, keys), block)
            for s in range(2):
                rows = slice(MID * s, MID * s + MID)
                back_send[2 * n + s] = att[rows].astype(BF16)
                back_lse_send[2 * n + s] = lse_rows(lse[rows], True)
        for who in near[:7]:
            pltpu.make_async_remote_copy(
                src_ref=back_send.at[who[1]], dst_ref=back_recv.at[inner], send_sem=back_ssem, recv_sem=back_rsem,
                device_id=who, device_id_type=MESH,
            ).start()
            pltpu.make_async_remote_copy(
                src_ref=back_lse_send.at[who[1]], dst_ref=back_lse_recv.at[inner],
                send_sem=lse_ssem.at[0], recv_sem=lse_rsem.at[0], device_id=who, device_id_type=MESH,
            ).start()
        back_recv[inner] = back_send[inner]
        back_lse_recv[inner] = back_lse_send[inner]

    def far():
        got = fq_recv.at[pl.ds(0, RG - 1)]
        pltpu.make_async_copy(got, got, fq_rsem).wait()
        stage[1, 0:256, :] = fq_recv[...].reshape(256, 128).astype(F32)
        got = kv_recv.at[pl.ds(0, GG - 1)]
        pltpu.make_async_copy(got, got, kv_rsem).wait()
        stage[0, 0:ROWS, :] = kv_recv[...].reshape(ROWS, 128).astype(F32)
        scores, blocks = [], []
        for p in range(PAIRS):
            q = jnp.concatenate([stage[1, pl.ds(2 * p + t, RG, stride=16), :] for t in range(FAR)], axis=0)
            k = jnp.concatenate([stage[0, pl.ds(2 * p + t, GG, stride=32), :] for t in range(FAR)], axis=0)
            v = jnp.concatenate([stage[0, pl.ds(16 + 2 * p + t, GG, stride=32), :] for t in range(FAR)], axis=0)
            scores.append(scores_of(q.astype(BF16), k.astype(BF16)))
            blocks.append(value_block(v.astype(BF16)))
        for p in range(PAIRS):
            att, lse = finish(scores[p], blocks[p])
            for t in range(FAR):
                far_att[pl.ds(2 * p + t, RG, stride=16), :] = att[RG * t : RG * t + RG]
                far_lse[pl.ds(2 * p + t, RG, stride=16), :] = lse[RG * t : RG * t + RG]
        for s in range(RG):
            far_send[s] = far_att[16 * s : 16 * s + 16, :].astype(BF16)
            far_lse_send[s] = lse_rows(far_lse[16 * s : 16 * s + 16, :], False)
        for who in near:
            its_y = who[1] % 2 * 2 + who[0] // 16
            pltpu.make_async_remote_copy(
                src_ref=far_send.at[its_y * 4 + who[1] // 2], dst_ref=far_recv.at[my_near],
                send_sem=far_ssem, recv_sem=far_rsem, device_id=who, device_id_type=MESH,
            ).start()
            pltpu.make_async_remote_copy(
                src_ref=far_lse_send.at[its_y * 4 + who[1] // 2], dst_ref=far_lse_recv.at[my_near],
                send_sem=lse_ssem.at[1], recv_sem=lse_rsem.at[1], device_id=who, device_id_type=MESH,
            ).start()
        far_recv[my_near] = far_send[my_near]
        far_lse_recv[my_near] = far_lse_send[my_near]

    def first_level(p):
        columns = pl.ds(pl.multiple_of(p * 128, 128), 128)
        keys = k_ref[:, columns]
        block = value_block(v_ref[:, columns])
        for c in range(4):
            rows = pl.ds(128 * c, 128)
            q = q_ref[rows, columns] * jnp.asarray(0.125, BF16)
            att, lse = finish(scores_of(q, keys), block)
            att_ref[p, rows, :] = att
            lse_pair[rows, :] = lse
        first_row = (2 * p) % 8
        one = lse_pair[pl.ds(first_row, MID, stride=8), :]
        two = lse_pair[pl.ds(first_row + 1, MID, stride=8), :]
        lse_ref[p] = jnp.where(second, two, one)

    events = (
        (opens, meet),
        (0, pick_all),
        (opens, send_mid),
        (at_along_early, send_along_early),
        (at_along_late, send_along_late),
        (at_mid, middle),
        (at_far, far),
    )

    def step(t, carry):
        for at, event in events:
            @pl.when(t == at)
            def _(event=event):
                event()

        @pl.when(jnp.logical_and(t > 0, t <= PAIRS))
        def _():
            first_level(t - 1)

        return carry

    lax.fori_loop(0, PAIRS + 2, step, 0)

    got = back_recv.at[pl.ds(0, INNER - 1)]
    pltpu.make_async_copy(got, got, back_rsem).wait()
    got = back_lse_recv.at[pl.ds(0, INNER - 1)]
    pltpu.make_async_copy(got, got, lse_rsem.at[0]).wait()
    mask = jnp.concatenate(diagonal(MID, 3, 0), axis=1)
    spread = half_sums(3 * 128)
    for p in range(PAIRS):
        first_row = (2 * p) % 8
        one = att_ref[p, pl.ds(first_row, MID, stride=8), :]
        two = att_ref[p, pl.ds(first_row + 1, MID, stride=8), :]
        lse1 = lse_ref[p]
        lse2 = jnp.where(mask, back_lse_recv[p], 0.0).astype(BF16)
        lse2 = jnp.dot(lse2, spread, preferred_element_type=F32)
        top = jnp.maximum(lse1, lse2)
        w1, w2 = jnp.exp(lse1 - top), jnp.exp(lse2 - top)
        total = w1 + w2
        merged = (w1 * jnp.where(second, two, one) + w2 * back_recv[p].astype(F32)) / total
        lse = top + jnp.log(total)
        for t in range(FAR):
            row = 32 * t + p // 4
            two_ref[0, 2 * p + t : 2 * p + t + 1, :] = merged[row : row + 1]
            two_ref[1, 2 * p + t : 2 * p + t + 1, :] = lse[row : row + 1]
        att_ref[p, pl.ds(first_row, MID, stride=8), :] = jnp.where(second, one, merged)
        att_ref[p, pl.ds(first_row + 1, MID, stride=8), :] = jnp.where(second, merged, two)
        merged_ref[:, 128 * p : 128 * p + 128] = att_ref[p, 0:ROWS, :].astype(BF16)

    sent = mid_send.at[pl.ds(0, INNER - 1)]
    pltpu.make_async_copy(sent, sent, mid_ssem).wait()
    sent = back_send.at[pl.ds(0, INNER - 1)]
    pltpu.make_async_copy(sent, sent, back_ssem).wait()
    sent = kv_recv.at[pl.ds(0, GG - 1)]
    pltpu.make_async_copy(sent, sent, kv_ssem).wait()
    sent = fq_recv.at[pl.ds(0, RG - 1)]
    pltpu.make_async_copy(sent, sent, fq_ssem).wait()
    sent = far_send.at[pl.ds(0, RG - 1)]
    pltpu.make_async_copy(sent, sent, far_ssem).wait()
    sent = back_lse_send.at[pl.ds(0, INNER - 1)]
    pltpu.make_async_copy(sent, sent, lse_ssem.at[0]).wait()
    sent = far_lse_send.at[pl.ds(0, RG - 1)]
    pltpu.make_async_copy(sent, sent, lse_ssem.at[1]).wait()

    got = far_recv.at[pl.ds(0, RG - 1)]
    pltpu.make_async_copy(got, got, far_rsem).wait()
    got = far_lse_recv.at[pl.ds(0, RG - 1)]
    pltpu.make_async_copy(got, got, lse_rsem.at[1]).wait()


def merge(merged_ref, two_ref, far_recv, far_lse_recv, out_hbm, edge, sem):
    copies = []
    for t in range(FAR):
        rest = pl.ds(256 * t + 16, 240)
        copies.append(pltpu.make_async_copy(merged_ref.at[rest, :], out_hbm.at[rest, :], sem.at[t]))
        copies[t].start()

    mask = diagonal(16, 3, 16)
    mask = jnp.logical_or(jnp.logical_or(mask[0], mask[1]), mask[2])
    partial_lse = jnp.concatenate([jnp.where(mask, far_lse_recv[s], 0.0) for s in range(RG)], axis=0).astype(BF16)
    partial_lse = jnp.dot(partial_lse, half_sums(128), preferred_element_type=F32)
    top = two_ref[1]
    for s in range(RG):
        top = jnp.maximum(top, partial_lse[16 * s : 16 * s + 16])
    weight = jnp.exp(two_ref[1] - top)
    numer = weight * two_ref[0]
    denom = weight
    for s in range(RG):
        weight = jnp.exp(partial_lse[16 * s : 16 * s + 16] - top)
        numer = numer + weight * far_recv[s].astype(F32)
        denom = denom + weight
    result = numer / denom

    row = lax.broadcasted_iota(jnp.int32, (16, 128), 0)
    half = lax.broadcasted_iota(jnp.int32, (16, 128), 1) // 64
    for t in range(FAR):
        for p in range(PAIRS):
            columns = slice(128 * p, 128 * p + 128)
            old = merged_ref[256 * t : 256 * t + 16, columns].astype(F32)
            new = jnp.where(row == 2 * p + half, result[2 * p + t : 2 * p + t + 1], old)
            edge[t, :, columns] = new.astype(BF16)
        copies.append(pltpu.make_async_copy(edge.at[t], out_hbm.at[pl.ds(256 * t, 16), :], sem.at[FAR + t]))
        copies[FAR + t].start()
    for copy in copies:
        copy.wait()


def on_device(queries, keys, values):
    dma = pltpu.SemaphoreType.DMA
    vmem = pltpu.VMEM
    results = pl.pallas_call(
        kernel,
        out_shape=[
            vmem((ROWS, 1024), BF16), vmem((2, 16, 128), F32), vmem((RG, 16, 128), BF16), vmem((RG, 1, 128), F32),
        ],
        in_specs=[pl.BlockSpec(memory_space=pltpu.HBM)] * 3,
        out_specs=[pl.BlockSpec(memory_space=pltpu.VMEM)] * 4,
        scratch_shapes=[
            vmem((ROWS, 1024), BF16), vmem((ROWS, 1024), BF16), vmem((ROWS, 1024), BF16),
            vmem((3, FAR, 16, 1024), BF16), dma((3,)), dma((3, FAR)),
            vmem((3, ROWS + 32, 128), F32), vmem((3, 16, 128), F32),
            vmem((INNER, 3 * MID, 128), BF16), vmem((INNER, 3 * MID, 128), BF16), dma, dma,
            vmem((INNER, MID, 128), BF16), vmem((INNER, MID, 128), BF16), dma, dma,
            vmem((INNER, 1, 384), F32), vmem((INNER, 1, 384), F32), vmem((RG, 1, 128), F32), dma((2,)), dma((2,)),
            vmem((32, 128), BF16), vmem((GG, 32, 128), BF16), dma, dma,
            vmem((16, 128), BF16), vmem((RG, 16, 128), BF16), dma, dma,
            vmem((RG, 16, 128), BF16), dma, dma,
            pltpu.SemaphoreType.REGULAR((2,)),
            vmem((PAIRS, ROWS + 8, 128), F32), vmem((ROWS + 8, 128), F32), vmem((PAIRS, MID, 128), F32),
            vmem((256 + 16, 128), F32), vmem((256 + 16, 128), F32),
        ],
        compiler_params=pltpu.CompilerParams(
            collective_id=0, has_side_effects=True, vmem_limit_bytes=40 * 1024 * 1024
        ),
    )(*(pltpu.with_memory_space_constraint(a, pltpu.HBM) for a in (queries, keys, values)))
    return pl.pallas_call(
        merge,
        out_shape=pltpu.HBM((ROWS, 1024), BF16),
        in_specs=[pl.BlockSpec(memory_space=pltpu.VMEM)] * 4,
        out_specs=pl.BlockSpec(memory_space=pltpu.HBM),
        scratch_shapes=[
            vmem((FAR, 16, 1024), BF16), dma((2 * FAR,)),
        ],
        compiler_params=pltpu.CompilerParams(vmem_limit_bytes=16 * 1024 * 1024),
    )(*(pltpu.with_memory_space_constraint(a, pltpu.VMEM) for a in results))


def solution(mesh):
    spec = P(("outer", "inner"), None)
    return jax.shard_map(
        on_device, mesh=mesh, in_specs=(spec, spec, spec), out_specs=spec, check_vma=False
    )
```

```python
import jax
import jax.numpy as jnp
from jax import lax
from jax.experimental import pallas as pl
from jax.experimental.pallas import tpu as pltpu
from jax.sharding import PartitionSpec as P

MESH = pl.DeviceIdType.MESH
F32 = jnp.float32
BF16 = jnp.bfloat16

ROWS = 512
PAIRS = 8
MID = 64
FAR = 2
INNER = 8
RG = 16
GG = 16
LOWEST = -1e30

INNER_STEPS = ((2, 2), (1, 2), (3, 2), (2, 0), (0, 2), (1, 0), (3, 0))
REST_STEPS = ((2, 1), (2, 3), (1, 1), (1, 3), (3, 1), (3, 3), (0, 1), (0, 3))


def lane_is_second(shape):
    return lax.broadcasted_iota(jnp.int32, shape, len(shape) - 1) >= 64


def split_pair(q):
    second = lane_is_second(q.shape)
    zero = jnp.zeros((), q.dtype)
    return jnp.concatenate([jnp.where(second, zero, q), jnp.where(second, q, zero)], axis=0)


def value_block(v):
    second = lane_is_second(v.shape)
    zero = jnp.zeros((), v.dtype)
    one = jnp.ones((), v.dtype)
    first = jnp.concatenate([jnp.where(second, zero, v), jnp.where(second, zero, one)], axis=1)
    other = jnp.concatenate([jnp.where(second, v, zero), jnp.where(second, one, zero)], axis=1)
    return jnp.concatenate([first, other], axis=0)


def scores_of(q, k):
    return lax.dot_general(split_pair(q), k, (((1,), (1,)), ((), ())), preferred_element_type=F32)


def finish(s, block):
    n = s.shape[0] // 2
    top = jnp.max(s, axis=1, keepdims=True)
    prob = jnp.exp(s - top).astype(BF16)
    both = jnp.concatenate([prob[:n], prob[n:]], axis=1)
    out = jnp.dot(both, block, preferred_element_type=F32)
    total = out[:, 128:]
    second = lane_is_second((n, 128))
    return out[:, :128] / total, jnp.where(second, top[n:], top[:n]) + jnp.log(total)


def parts_of(x):
    high = x.astype(BF16)
    rest = x - high.astype(F32)
    mid = rest.astype(BF16)
    return high, mid, (rest - mid.astype(F32)).astype(BF16)


def diagonal(rows, parts, width):
    row = lax.broadcasted_iota(jnp.int32, (rows, 128), 0)
    lane = lax.broadcasted_iota(jnp.int32, (rows, 128), 1) % 64
    return [lane == row + t * width for t in range(parts)]


def lse_rows(lse, wide):
    n = lse.shape[0]
    masks = diagonal(n, 3, 0 if wide else 16)
    picked = [
        jnp.sum(jnp.where(mask, part.astype(F32), 0.0), axis=0, keepdims=True)
        for mask, part in zip(masks, parts_of(lse), strict=True)
    ]
    return jnp.concatenate(picked, axis=1) if wide else picked[0] + picked[1] + picked[2]


def half_sums(width):
    row = lax.broadcasted_iota(jnp.int32, (width, 128), 0)
    lane = lax.broadcasted_iota(jnp.int32, (width, 128), 1)
    return jnp.where(row % 128 // 64 == lane // 64, 1.0, 0.0).astype(BF16)


def kernel(
    q_hbm, k_hbm, v_hbm, merged_ref, two_ref, far_recv, far_lse_recv,
    q_ref, k_ref, v_ref, edge, load_sem, edge_sem,
    stage, far_stage, mid_send, mid_recv, mid_ssem, mid_rsem,
    back_send, back_recv, back_ssem, back_rsem, back_lse_send, back_lse_recv, far_lse_send, lse_ssem, lse_rsem,
    kv_send, kv_recv, kv_ssem, kv_rsem,
    fq_send, fq_recv, fq_ssem, fq_rsem,
    far_send, far_ssem, far_rsem,
    along_sem, att_ref, lse_pair, lse_ref, far_att, far_lse,
):
    outer = lax.axis_index("outer")
    inner = lax.axis_index("inner")
    core = outer % 2
    z = (outer // 2) % 8
    y_lo = outer // 16
    x = inner // 2
    y_hi = inner % 2

    y = y_hi * 2 + y_lo

    def outer_id(y_lo, z, core):
        return y_lo * 16 + z * 2 + core

    near, along = [], []
    for dx, dy in INNER_STEPS + REST_STEPS:
        px, py = (x + dx) % 4, (y + dy) % 4
        near.append((outer_id(py % 2, z, core), px * 2 + py // 2))
    wave = jnp.minimum(z, 4)
    for pz in range(8):
        for pc in range(2):
            here = jnp.logical_and(z == pz, core == pc)
            later = jnp.where(here, 9, min(pz, 4) - wave)
            along.append(((outer_id(y_lo, pz, pc), inner), later, pz))
    early_along = jnp.where(z < 4, 2 * z + 1, 15)

    entry = sum(9 * v - 2 * (v // 2) - 11 * (v // 3) for v in (x, y))
    opens = jnp.where(entry < 20, 1, 0)
    at_mid = 6 + opens + jnp.where(entry < 5, 1, 0)
    at_far = at_mid
    at_along_early = jnp.where(z < 3, 4 + opens - z, -1)
    at_along_late = jnp.where(z < 4, at_mid - wave + wave // 3, -1)

    barrier = pltpu.get_barrier_semaphore()
    for who in near:
        pl.semaphore_signal(barrier, 1, device_id=who, device_id_type=MESH)
    for who, later, _ in along:
        @pl.when(jnp.logical_and(later >= 0, later < 9))
        def _(who=who):
            pl.semaphore_signal(barrier, 1, device_id=who, device_id_type=MESH)

    edges = []
    for a, src in ((1, k_hbm), (2, v_hbm), (0, q_hbm)):
        for t in range(FAR):
            copy = pltpu.make_async_copy(src.at[pl.ds(256 * t, 16), :], edge.at[a, t], edge_sem.at[a, t])
            copy.start()
            edges.append(copy)
    loads = []
    for a, (src, dst) in enumerate(((q_hbm, q_ref), (k_hbm, k_ref), (v_hbm, v_ref))):
        copy = pltpu.make_async_copy(src, dst, load_sem.at[a])
        copy.start()
        loads.append(copy)

    row16 = lax.broadcasted_iota(jnp.int32, (16, 1024), 0)
    head16 = lax.broadcasted_iota(jnp.int32, (16, 1024), 1) // 64
    my_near = y * 4 + x
    my_along = z * 2 + core

    def pick_edge(a):
        for t in range(FAR):
            block = edge[a, t].astype(F32)
            picked = jnp.sum(jnp.where(row16 == head16, block, 0.0), axis=0, keepdims=True)
            for p in range(PAIRS):
                far_stage[a, pl.ds(2 * p + t, 1), :] = picked[:, 128 * p : 128 * p + 128]

    def kv_copy(who):
        return pltpu.make_async_remote_copy(
            src_ref=kv_send, dst_ref=kv_recv.at[my_along], send_sem=kv_ssem, recv_sem=kv_rsem,
            device_id=who, device_id_type=MESH,
        )

    def fq_copy(who):
        return pltpu.make_async_remote_copy(
            src_ref=fq_send, dst_ref=fq_recv.at[my_near], send_sem=fq_ssem, recv_sem=fq_rsem,
            device_id=who, device_id_type=MESH,
        )

    def mid_copy(who):
        return pltpu.make_async_remote_copy(
            src_ref=mid_send.at[who[1]], dst_ref=mid_recv.at[inner], send_sem=mid_ssem, recv_sem=mid_rsem,
            device_id=who, device_id_type=MESH,
        )

    for copy in edges[:4]:
        copy.wait()
    pick_edge(1)
    pick_edge(2)
    kv_send[0:16, :] = far_stage[1].astype(BF16)
    kv_send[16:32, :] = far_stage[2].astype(BF16)
    kv_recv[my_along] = kv_send[...]
    second = lane_is_second((MID, 128))

    def pick(p):
        first_row = (2 * p) % 8
        columns = pl.ds(pl.multiple_of(p * 128, 128), 128)
        for a, ref in enumerate((q_ref, k_ref, v_ref)):
            wide = ref[:, columns].astype(F32)
            if a == 0:
                wide = wide * 0.125
            stage[a, 0:ROWS, :] = wide
        for a in range(3):
            one = stage[a, pl.ds(first_row, MID, stride=8), :]
            two = stage[a, pl.ds(first_row + 1, MID, stride=8), :]
            mid_send[p, pl.ds(MID * a, MID), :] = jnp.where(second, two, one).astype(BF16)


    def pick_all():
        for copy in loads:
            copy.wait()
        for who in near[:7]:
            pick(who[1])

            @pl.when(opens == 0)
            def _(who=who):
                mid_copy(who).start()
        pick(inner)
        mid_recv[inner] = mid_send[inner]

    def meet():
        pl.semaphore_wait(barrier, 15 + early_along)
        for who, later, _ in along:
            @pl.when(later < 0)
            def _(who=who):
                kv_copy(who).start()
        for who, later, _ in along:
            @pl.when(later < 0)
            def _(who=who):
                pl.semaphore_signal(along_sem.at[jnp.where(z < 4, 0, 1)], 1, device_id=who, device_id_type=MESH)
        for who, later, _ in along:
            @pl.when(later == 0)
            def _(who=who):
                kv_copy(who).start()

    def send_mid():
        @pl.when(opens > 0)
        def _():
            for who in near[:7]:
                mid_copy(who).start()

        for copy in edges[4:]:
            copy.wait()
        pick_edge(0)
        fq_send[...] = (far_stage[0] * 0.125).astype(BF16)
        fq_recv[my_near] = fq_send[...]
        for who in near:
            fq_copy(who).start()

    def send_along(half):
        for who, later, pz in along[8 * half : 8 * half + 8]:
            @pl.when(jnp.logical_and(later > 0, later < 9))
            def _(who=who):
                kv_copy(who).start()

    def send_along_early():
        pl.semaphore_wait(along_sem.at[0], 6 - 2 * z)
        send_along(0)

    def send_along_late():
        pl.semaphore_wait(along_sem.at[1], 8)
        send_along(1)

    def middle():
        got = mid_recv.at[pl.ds(0, INNER - 1)]
        pltpu.make_async_copy(got, got, mid_rsem).wait()
        keys = mid_recv[:, MID : 2 * MID, :].reshape(ROWS, 128)
        block = value_block(mid_recv[:, 2 * MID :, :].reshape(ROWS, 128))
        for n in range(4):
            q = mid_recv[2 * n : 2 * n + 2, 0:MID, :].reshape(2 * MID, 128)
            att, lse = finish(scores_of(q, keys), block)
            for s in range(2):
                rows = slice(MID * s, MID * s + MID)
                back_send[2 * n + s] = att[rows].astype(BF16)
                back_lse_send[2 * n + s] = lse_rows(lse[rows], True)
        for who in near[:7]:
            pltpu.make_async_remote_copy(
                src_ref=back_send.at[who[1]], dst_ref=back_recv.at[inner], send_sem=back_ssem, recv_sem=back_rsem,
                device_id=who, device_id_type=MESH,
            ).start()
            pltpu.make_async_remote_copy(
                src_ref=back_lse_send.at[who[1]], dst_ref=back_lse_recv.at[inner],
                send_sem=lse_ssem.at[0], recv_sem=lse_rsem.at[0], device_id=who, device_id_type=MESH,
            ).start()
        back_recv[inner] = back_send[inner]
        back_lse_recv[inner] = back_lse_send[inner]

    def far():
        got = fq_recv.at[pl.ds(0, RG - 1)]
        pltpu.make_async_copy(got, got, fq_rsem).wait()
        stage[1, 0:256, :] = fq_recv[...].reshape(256, 128).astype(F32)
        got = kv_recv.at[pl.ds(0, GG - 1)]
        pltpu.make_async_copy(got, got, kv_rsem).wait()
        stage[0, 0:ROWS, :] = kv_recv[...].reshape(ROWS, 128).astype(F32)
        scores, blocks = [], []
        for p in range(PAIRS):
            q = jnp.concatenate([stage[1, pl.ds(2 * p + t, RG, stride=16), :] for t in range(FAR)], axis=0)
            k = jnp.concatenate([stage[0, pl.ds(2 * p + t, GG, stride=32), :] for t in range(FAR)], axis=0)
            v = jnp.concatenate([stage[0, pl.ds(16 + 2 * p + t, GG, stride=32), :] for t in range(FAR)], axis=0)
            scores.append(scores_of(q.astype(BF16), k.astype(BF16)))
            blocks.append(value_block(v.astype(BF16)))
        for p in range(PAIRS):
            att, lse = finish(scores[p], blocks[p])
            for t in range(FAR):
                far_att[pl.ds(2 * p + t, RG, stride=16), :] = att[RG * t : RG * t + RG]
                far_lse[pl.ds(2 * p + t, RG, stride=16), :] = lse[RG * t : RG * t + RG]
        for s in range(RG):
            far_send[s] = far_att[16 * s : 16 * s + 16, :].astype(BF16)
            far_lse_send[s] = lse_rows(far_lse[16 * s : 16 * s + 16, :], False)
        for who in near:
            its_y = who[1] % 2 * 2 + who[0] // 16
            pltpu.make_async_remote_copy(
                src_ref=far_send.at[its_y * 4 + who[1] // 2], dst_ref=far_recv.at[my_near],
                send_sem=far_ssem, recv_sem=far_rsem, device_id=who, device_id_type=MESH,
            ).start()
            pltpu.make_async_remote_copy(
                src_ref=far_lse_send.at[its_y * 4 + who[1] // 2], dst_ref=far_lse_recv.at[my_near],
                send_sem=lse_ssem.at[1], recv_sem=lse_rsem.at[1], device_id=who, device_id_type=MESH,
            ).start()
        far_recv[my_near] = far_send[my_near]
        far_lse_recv[my_near] = far_lse_send[my_near]

    def first_level(p):
        columns = pl.ds(pl.multiple_of(p * 128, 128), 128)
        keys = k_ref[:, columns]
        block = value_block(v_ref[:, columns])
        for c in range(4):
            rows = pl.ds(128 * c, 128)
            q = q_ref[rows, columns] * jnp.asarray(0.125, BF16)
            att, lse = finish(scores_of(q, keys), block)
            att_ref[p, rows, :] = att
            lse_pair[rows, :] = lse
        first_row = (2 * p) % 8
        one = lse_pair[pl.ds(first_row, MID, stride=8), :]
        two = lse_pair[pl.ds(first_row + 1, MID, stride=8), :]
        lse_ref[p] = jnp.where(second, two, one)

    events = (
        (opens, meet),
        (0, pick_all),
        (opens, send_mid),
        (at_along_early, send_along_early),
        (at_along_late, send_along_late),
        (at_mid, middle),
        (at_far, far),
    )

    def step(t, carry):
        for at, event in events:
            @pl.when(t == at)
            def _(event=event):
                event()

        @pl.when(jnp.logical_and(t > 0, t <= PAIRS))
        def _():
            first_level(t - 1)

        return carry

    lax.fori_loop(0, PAIRS + 2, step, 0)

    got = back_recv.at[pl.ds(0, INNER - 1)]
    pltpu.make_async_copy(got, got, back_rsem).wait()
    got = back_lse_recv.at[pl.ds(0, INNER - 1)]
    pltpu.make_async_copy(got, got, lse_rsem.at[0]).wait()
    mask = jnp.concatenate(diagonal(MID, 3, 0), axis=1)
    spread = half_sums(3 * 128)
    for p in range(PAIRS):
        first_row = (2 * p) % 8
        one = att_ref[p, pl.ds(first_row, MID, stride=8), :]
        two = att_ref[p, pl.ds(first_row + 1, MID, stride=8), :]
        lse1 = lse_ref[p]
        lse2 = jnp.where(mask, back_lse_recv[p], 0.0).astype(BF16)
        lse2 = jnp.dot(lse2, spread, preferred_element_type=F32)
        top = jnp.maximum(lse1, lse2)
        w1, w2 = jnp.exp(lse1 - top), jnp.exp(lse2 - top)
        total = w1 + w2
        merged = (w1 * jnp.where(second, two, one) + w2 * back_recv[p].astype(F32)) / total
        lse = top + jnp.log(total)
        for t in range(FAR):
            row = 32 * t + p // 4
            two_ref[0, 2 * p + t : 2 * p + t + 1, :] = merged[row : row + 1]
            two_ref[1, 2 * p + t : 2 * p + t + 1, :] = lse[row : row + 1]
        att_ref[p, pl.ds(first_row, MID, stride=8), :] = jnp.where(second, one, merged)
        att_ref[p, pl.ds(first_row + 1, MID, stride=8), :] = jnp.where(second, merged, two)
        merged_ref[:, 128 * p : 128 * p + 128] = att_ref[p, 0:ROWS, :].astype(BF16)

    sent = mid_send.at[pl.ds(0, INNER - 1)]
    pltpu.make_async_copy(sent, sent, mid_ssem).wait()
    sent = back_send.at[pl.ds(0, INNER - 1)]
    pltpu.make_async_copy(sent, sent, back_ssem).wait()
    sent = kv_recv.at[pl.ds(0, GG - 1)]
    pltpu.make_async_copy(sent, sent, kv_ssem).wait()
    sent = fq_recv.at[pl.ds(0, RG - 1)]
    pltpu.make_async_copy(sent, sent, fq_ssem).wait()
    sent = far_send.at[pl.ds(0, RG - 1)]
    pltpu.make_async_copy(sent, sent, far_ssem).wait()
    sent = back_lse_send.at[pl.ds(0, INNER - 1)]
    pltpu.make_async_copy(sent, sent, lse_ssem.at[0]).wait()
    sent = far_lse_send.at[pl.ds(0, RG - 1)]
    pltpu.make_async_copy(sent, sent, lse_ssem.at[1]).wait()

    got = far_recv.at[pl.ds(0, RG - 1)]
    pltpu.make_async_copy(got, got, far_rsem).wait()
    got = far_lse_recv.at[pl.ds(0, RG - 1)]
    pltpu.make_async_copy(got, got, lse_rsem.at[1]).wait()


def merge(merged_ref, two_ref, far_recv, far_lse_recv, out_hbm, edge, sem):
    copies = []
    for t in range(FAR):
        rest = pl.ds(256 * t + 16, 240)
        copies.append(pltpu.make_async_copy(merged_ref.at[rest, :], out_hbm.at[rest, :], sem.at[t]))
        copies[t].start()

    mask = diagonal(16, 3, 16)
    mask = jnp.logical_or(jnp.logical_or(mask[0], mask[1]), mask[2])
    partial_lse = jnp.concatenate([jnp.where(mask, far_lse_recv[s], 0.0) for s in range(RG)], axis=0).astype(BF16)
    partial_lse = jnp.dot(partial_lse, half_sums(128), preferred_element_type=F32)
    top = two_ref[1]
    for s in range(RG):
        top = jnp.maximum(top, partial_lse[16 * s : 16 * s + 16])
    weight = jnp.exp(two_ref[1] - top)
    numer = weight * two_ref[0]
    denom = weight
    for s in range(RG):
        weight = jnp.exp(partial_lse[16 * s : 16 * s + 16] - top)
        numer = numer + weight * far_recv[s].astype(F32)
        denom = denom + weight
    result = numer / denom

    row = lax.broadcasted_iota(jnp.int32, (16, 128), 0)
    half = lax.broadcasted_iota(jnp.int32, (16, 128), 1) // 64
    for t in range(FAR):
        for p in range(PAIRS):
            columns = slice(128 * p, 128 * p + 128)
            old = merged_ref[256 * t : 256 * t + 16, columns].astype(F32)
            new = jnp.where(row == 2 * p + half, result[2 * p + t : 2 * p + t + 1], old)
            edge[t, :, columns] = new.astype(BF16)
        copies.append(pltpu.make_async_copy(edge.at[t], out_hbm.at[pl.ds(256 * t, 16), :], sem.at[FAR + t]))
        copies[FAR + t].start()
    for copy in copies:
        copy.wait()


def on_device(queries, keys, values):
    dma = pltpu.SemaphoreType.DMA
    vmem = pltpu.VMEM
    results = pl.pallas_call(
        kernel,
        out_shape=[
            vmem((ROWS, 1024), BF16), vmem((2, 16, 128), F32), vmem((RG, 16, 128), BF16), vmem((RG, 1, 128), F32),
        ],
        in_specs=[pl.BlockSpec(memory_space=pltpu.HBM)] * 3,
        out_specs=[pl.BlockSpec(memory_space=pltpu.VMEM)] * 4,
        scratch_shapes=[
            vmem((ROWS, 1024), BF16), vmem((ROWS, 1024), BF16), vmem((ROWS, 1024), BF16),
            vmem((3, FAR, 16, 1024), BF16), dma((3,)), dma((3, FAR)),
            vmem((3, ROWS + 32, 128), F32), vmem((3, 16, 128), F32),
            vmem((INNER, 3 * MID, 128), BF16), vmem((INNER, 3 * MID, 128), BF16), dma, dma,
            vmem((INNER, MID, 128), BF16), vmem((INNER, MID, 128), BF16), dma, dma,
            vmem((INNER, 1, 384), F32), vmem((INNER, 1, 384), F32), vmem((RG, 1, 128), F32), dma((2,)), dma((2,)),
            vmem((32, 128), BF16), vmem((GG, 32, 128), BF16), dma, dma,
            vmem((16, 128), BF16), vmem((RG, 16, 128), BF16), dma, dma,
            vmem((RG, 16, 128), BF16), dma, dma,
            pltpu.SemaphoreType.REGULAR((2,)),
            vmem((PAIRS, ROWS + 8, 128), F32), vmem((ROWS + 8, 128), F32), vmem((PAIRS, MID, 128), F32),
            vmem((256 + 16, 128), F32), vmem((256 + 16, 128), F32),
        ],
        compiler_params=pltpu.CompilerParams(
            collective_id=0, has_side_effects=True, vmem_limit_bytes=40 * 1024 * 1024
        ),
    )(*(pltpu.with_memory_space_constraint(a, pltpu.HBM) for a in (queries, keys, values)))
    return pl.pallas_call(
        merge,
        out_shape=pltpu.HBM((ROWS, 1024), BF16),
        in_specs=[pl.BlockSpec(memory_space=pltpu.VMEM)] * 4,
        out_specs=pl.BlockSpec(memory_space=pltpu.HBM),
        scratch_shapes=[
            vmem((FAR, 16, 1024), BF16), dma((2 * FAR,)),
        ],
        compiler_params=pltpu.CompilerParams(vmem_limit_bytes=16 * 1024 * 1024),
    )(*(pltpu.with_memory_space_constraint(a, pltpu.VMEM) for a in results))


def solution(mesh):
    spec = P(("outer", "inner"), None)
    return jax.shard_map(
        on_device, mesh=mesh, in_specs=(spec, spec, spec), out_specs=spec, check_vma=False
    )
```

```python
import jax
import jax.numpy as jnp
from jax import lax
from jax.experimental import pallas as pl
from jax.experimental.pallas import tpu as pltpu
from jax.sharding import PartitionSpec as P

MESH = pl.DeviceIdType.MESH
F32 = jnp.float32
BF16 = jnp.bfloat16

ROWS = 512
PAIRS = 8
MID = 64
FAR = 2
INNER = 8
RG = 16
GG = 16
LOWEST = -1e30

INNER_STEPS = ((2, 2), (1, 2), (3, 2), (2, 0), (0, 2), (1, 0), (3, 0))
REST_STEPS = ((2, 1), (2, 3), (1, 1), (1, 3), (3, 1), (3, 3), (0, 1), (0, 3))


def lane_is_second(shape):
    return lax.broadcasted_iota(jnp.int32, shape, len(shape) - 1) >= 64


def split_pair(q):
    second = lane_is_second(q.shape)
    zero = jnp.zeros((), q.dtype)
    return jnp.concatenate([jnp.where(second, zero, q), jnp.where(second, q, zero)], axis=0)


def value_block(v):
    second = lane_is_second(v.shape)
    zero = jnp.zeros((), v.dtype)
    one = jnp.ones((), v.dtype)
    first = jnp.concatenate([jnp.where(second, zero, v), jnp.where(second, zero, one)], axis=1)
    other = jnp.concatenate([jnp.where(second, v, zero), jnp.where(second, one, zero)], axis=1)
    return jnp.concatenate([first, other], axis=0)


def scores_of(q, k):
    return lax.dot_general(split_pair(q), k, (((1,), (1,)), ((), ())), preferred_element_type=F32)


def finish(s, block):
    n = s.shape[0] // 2
    top = jnp.max(s, axis=1, keepdims=True)
    prob = jnp.exp(s - top).astype(BF16)
    both = jnp.concatenate([prob[:n], prob[n:]], axis=1)
    out = jnp.dot(both, block, preferred_element_type=F32)
    total = out[:, 128:]
    second = lane_is_second((n, 128))
    return out[:, :128] / total, jnp.where(second, top[n:], top[:n]) + jnp.log(total)


def parts_of(x):
    high = x.astype(BF16)
    rest = x - high.astype(F32)
    mid = rest.astype(BF16)
    return high, mid, (rest - mid.astype(F32)).astype(BF16)


def diagonal(rows, parts, width):
    row = lax.broadcasted_iota(jnp.int32, (rows, 128), 0)
    lane = lax.broadcasted_iota(jnp.int32, (rows, 128), 1) % 64
    return [lane == row + t * width for t in range(parts)]


def lse_rows(lse, wide):
    n = lse.shape[0]
    masks = diagonal(n, 3, 0 if wide else 16)
    picked = [
        jnp.sum(jnp.where(mask, part.astype(F32), 0.0), axis=0, keepdims=True)
        for mask, part in zip(masks, parts_of(lse), strict=True)
    ]
    return jnp.concatenate(picked, axis=1) if wide else picked[0] + picked[1] + picked[2]


def half_sums(width):
    row = lax.broadcasted_iota(jnp.int32, (width, 128), 0)
    lane = lax.broadcasted_iota(jnp.int32, (width, 128), 1)
    return jnp.where(row % 128 // 64 == lane // 64, 1.0, 0.0).astype(BF16)


def kernel(
    q_hbm, k_hbm, v_hbm, merged_ref, two_ref, far_recv, far_lse_recv,
    q_ref, k_ref, v_ref, edge, load_sem, edge_sem,
    stage, far_stage, mid_send, mid_recv, mid_ssem, mid_rsem,
    back_send, back_recv, back_ssem, back_rsem, back_lse_send, back_lse_recv, far_lse_send, lse_ssem, lse_rsem,
    kv_send, kv_recv, kv_ssem, kv_rsem,
    fq_send, fq_recv, fq_ssem, fq_rsem,
    far_send, far_ssem, far_rsem,
    along_sem, att_ref, lse_pair, lse_ref, far_att, far_lse,
):
    outer = lax.axis_index("outer")
    inner = lax.axis_index("inner")
    core = outer % 2
    z = (outer // 2) % 8
    y_lo = outer // 16
    x = inner // 2
    y_hi = inner % 2

    y = y_hi * 2 + y_lo

    def outer_id(y_lo, z, core):
        return y_lo * 16 + z * 2 + core

    near, along = [], []
    for dx, dy in INNER_STEPS + REST_STEPS:
        px, py = (x + dx) % 4, (y + dy) % 4
        near.append((outer_id(py % 2, z, core), px * 2 + py // 2))
    wave = jnp.minimum(z, 4)
    for pz in range(8):
        for pc in range(2):
            here = jnp.logical_and(z == pz, core == pc)
            later = jnp.where(here, 9, min(pz, 4) - wave)
            along.append(((outer_id(y_lo, pz, pc), inner), later, pz))
    early_along = jnp.where(z < 4, 2 * z + 1, 15)

    entry = sum(9 * v - 2 * (v // 2) - 11 * (v // 3) for v in (x, y))
    opens = jnp.where(entry < 20, 1, 0)
    at_mid = 6 + opens + jnp.where(entry < 5, 1, 0)
    at_far = at_mid
    at_along_early = jnp.where(z < 3, 4 + opens - z, -1)
    at_along_late = jnp.where(z < 4, at_mid - wave + wave // 3, -1)

    barrier = pltpu.get_barrier_semaphore()
    def speak_along(peers):
        for who, later, _ in peers:
            @pl.when(jnp.logical_and(later >= 0, later < 9))
            def _(who=who):
                pl.semaphore_signal(barrier, 1, device_id=who, device_id_type=MESH)

    @pl.when(z >= 4)
    def _():
        speak_along(along[8:])

    for who in near:
        pl.semaphore_signal(barrier, 1, device_id=who, device_id_type=MESH)

    @pl.when(z < 4)
    def _():
        speak_along(along)

    edges = []
    for a, src in ((1, k_hbm), (2, v_hbm), (0, q_hbm)):
        for t in range(FAR):
            copy = pltpu.make_async_copy(src.at[pl.ds(256 * t, 16), :], edge.at[a, t], edge_sem.at[a, t])
            copy.start()
            edges.append(copy)
    loads = []
    for a, (src, dst) in enumerate(((q_hbm, q_ref), (k_hbm, k_ref), (v_hbm, v_ref))):
        copy = pltpu.make_async_copy(src, dst, load_sem.at[a])
        copy.start()
        loads.append(copy)

    row16 = lax.broadcasted_iota(jnp.int32, (16, 1024), 0)
    head16 = lax.broadcasted_iota(jnp.int32, (16, 1024), 1) // 64
    my_near = y * 4 + x
    my_along = z * 2 + core

    def pick_edge(a):
        for t in range(FAR):
            block = edge[a, t].astype(F32)
            picked = jnp.sum(jnp.where(row16 == head16, block, 0.0), axis=0, keepdims=True)
            for p in range(PAIRS):
                far_stage[a, pl.ds(2 * p + t, 1), :] = picked[:, 128 * p : 128 * p + 128]

    def kv_copy(who):
        return pltpu.make_async_remote_copy(
            src_ref=kv_send, dst_ref=kv_recv.at[my_along], send_sem=kv_ssem, recv_sem=kv_rsem,
            device_id=who, device_id_type=MESH,
        )

    def fq_copy(who):
        return pltpu.make_async_remote_copy(
            src_ref=fq_send, dst_ref=fq_recv.at[my_near], send_sem=fq_ssem, recv_sem=fq_rsem,
            device_id=who, device_id_type=MESH,
        )

    def mid_copy(who):
        return pltpu.make_async_remote_copy(
            src_ref=mid_send.at[who[1]], dst_ref=mid_recv.at[inner], send_sem=mid_ssem, recv_sem=mid_rsem,
            device_id=who, device_id_type=MESH,
        )

    for copy in edges[:4]:
        copy.wait()
    pick_edge(1)
    pick_edge(2)
    kv_send[0:16, :] = far_stage[1].astype(BF16)
    kv_send[16:32, :] = far_stage[2].astype(BF16)
    kv_recv[my_along] = kv_send[...]
    second = lane_is_second((MID, 128))

    def pick(p):
        first_row = (2 * p) % 8
        columns = pl.ds(pl.multiple_of(p * 128, 128), 128)
        for a, ref in enumerate((q_ref, k_ref, v_ref)):
            wide = ref[:, columns].astype(F32)
            if a == 0:
                wide = wide * 0.125
            stage[a, 0:ROWS, :] = wide
        for a in range(3):
            one = stage[a, pl.ds(first_row, MID, stride=8), :]
            two = stage[a, pl.ds(first_row + 1, MID, stride=8), :]
            mid_send[p, pl.ds(MID * a, MID), :] = jnp.where(second, two, one).astype(BF16)


    def pick_all():
        for copy in loads:
            copy.wait()
        for who in near[:7]:
            pick(who[1])

            @pl.when(opens == 0)
            def _(who=who):
                mid_copy(who).start()
        pick(inner)
        mid_recv[inner] = mid_send[inner]

    def meet():
        pl.semaphore_wait(barrier, 15 + early_along)
        for who, later, _ in along:
            @pl.when(later < 0)
            def _(who=who):
                kv_copy(who).start()
        for who, later, _ in along:
            @pl.when(later < 0)
            def _(who=who):
                pl.semaphore_signal(along_sem.at[jnp.where(z < 4, 0, 1)], 1, device_id=who, device_id_type=MESH)
        for who, later, _ in along:
            @pl.when(later == 0)
            def _(who=who):
                kv_copy(who).start()

    def send_mid():
        @pl.when(opens > 0)
        def _():
            for who in near[:7]:
                mid_copy(who).start()

        for copy in edges[4:]:
            copy.wait()
        pick_edge(0)
        fq_send[...] = (far_stage[0] * 0.125).astype(BF16)
        fq_recv[my_near] = fq_send[...]
        for who in near:
            fq_copy(who).start()

    def send_along(half):
        for who, later, pz in along[8 * half : 8 * half + 8]:
            @pl.when(jnp.logical_and(later > 0, later < 9))
            def _(who=who):
                kv_copy(who).start()

    def send_along_early():
        pl.semaphore_wait(along_sem.at[0], 6 - 2 * z)
        send_along(0)

    def send_along_late():
        pl.semaphore_wait(along_sem.at[1], 8)
        send_along(1)

    def middle():
        got = mid_recv.at[pl.ds(0, INNER - 1)]
        pltpu.make_async_copy(got, got, mid_rsem).wait()
        keys = mid_recv[:, MID : 2 * MID, :].reshape(ROWS, 128)
        block = value_block(mid_recv[:, 2 * MID :, :].reshape(ROWS, 128))
        for n in range(4):
            q = mid_recv[2 * n : 2 * n + 2, 0:MID, :].reshape(2 * MID, 128)
            att, lse = finish(scores_of(q, keys), block)
            for s in range(2):
                rows = slice(MID * s, MID * s + MID)
                back_send[2 * n + s] = att[rows].astype(BF16)
                back_lse_send[2 * n + s] = lse_rows(lse[rows], True)
        for who in near[:7]:
            pltpu.make_async_remote_copy(
                src_ref=back_send.at[who[1]], dst_ref=back_recv.at[inner], send_sem=back_ssem, recv_sem=back_rsem,
                device_id=who, device_id_type=MESH,
            ).start()
            pltpu.make_async_remote_copy(
                src_ref=back_lse_send.at[who[1]], dst_ref=back_lse_recv.at[inner],
                send_sem=lse_ssem.at[0], recv_sem=lse_rsem.at[0], device_id=who, device_id_type=MESH,
            ).start()
        back_recv[inner] = back_send[inner]
        back_lse_recv[inner] = back_lse_send[inner]

    def far():
        got = fq_recv.at[pl.ds(0, RG - 1)]
        pltpu.make_async_copy(got, got, fq_rsem).wait()
        stage[1, 0:256, :] = fq_recv[...].reshape(256, 128).astype(F32)
        got = kv_recv.at[pl.ds(0, GG - 1)]
        pltpu.make_async_copy(got, got, kv_rsem).wait()
        stage[0, 0:ROWS, :] = kv_recv[...].reshape(ROWS, 128).astype(F32)
        scores, blocks = [], []
        for p in range(PAIRS):
            q = jnp.concatenate([stage[1, pl.ds(2 * p + t, RG, stride=16), :] for t in range(FAR)], axis=0)
            k = jnp.concatenate([stage[0, pl.ds(2 * p + t, GG, stride=32), :] for t in range(FAR)], axis=0)
            v = jnp.concatenate([stage[0, pl.ds(16 + 2 * p + t, GG, stride=32), :] for t in range(FAR)], axis=0)
            scores.append(scores_of(q.astype(BF16), k.astype(BF16)))
            blocks.append(value_block(v.astype(BF16)))
        for p in range(PAIRS):
            att, lse = finish(scores[p], blocks[p])
            for t in range(FAR):
                far_att[pl.ds(2 * p + t, RG, stride=16), :] = att[RG * t : RG * t + RG]
                far_lse[pl.ds(2 * p + t, RG, stride=16), :] = lse[RG * t : RG * t + RG]
        for s in range(RG):
            far_send[s] = far_att[16 * s : 16 * s + 16, :].astype(BF16)
            far_lse_send[s] = lse_rows(far_lse[16 * s : 16 * s + 16, :], False)
        for who in near:
            its_y = who[1] % 2 * 2 + who[0] // 16
            pltpu.make_async_remote_copy(
                src_ref=far_send.at[its_y * 4 + who[1] // 2], dst_ref=far_recv.at[my_near],
                send_sem=far_ssem, recv_sem=far_rsem, device_id=who, device_id_type=MESH,
            ).start()
            pltpu.make_async_remote_copy(
                src_ref=far_lse_send.at[its_y * 4 + who[1] // 2], dst_ref=far_lse_recv.at[my_near],
                send_sem=lse_ssem.at[1], recv_sem=lse_rsem.at[1], device_id=who, device_id_type=MESH,
            ).start()
        far_recv[my_near] = far_send[my_near]
        far_lse_recv[my_near] = far_lse_send[my_near]

    def first_level(p):
        columns = pl.ds(pl.multiple_of(p * 128, 128), 128)
        keys = k_ref[:, columns]
        block = value_block(v_ref[:, columns])
        for c in range(4):
            rows = pl.ds(128 * c, 128)
            q = q_ref[rows, columns] * jnp.asarray(0.125, BF16)
            att, lse = finish(scores_of(q, keys), block)
            att_ref[p, rows, :] = att
            lse_pair[rows, :] = lse
        first_row = (2 * p) % 8
        one = lse_pair[pl.ds(first_row, MID, stride=8), :]
        two = lse_pair[pl.ds(first_row + 1, MID, stride=8), :]
        lse_ref[p] = jnp.where(second, two, one)

    events = (
        (opens, meet),
        (0, pick_all),
        (opens, send_mid),
        (at_along_early, send_along_early),
        (at_along_late, send_along_late),
        (at_mid, middle),
        (at_far, far),
    )

    def step(t, carry):
        for at, event in events:
            @pl.when(t == at)
            def _(event=event):
                event()

        @pl.when(jnp.logical_and(t > 0, t <= PAIRS))
        def _():
            first_level(t - 1)

        return carry

    lax.fori_loop(0, PAIRS + 2, step, 0)

    got = back_recv.at[pl.ds(0, INNER - 1)]
    pltpu.make_async_copy(got, got, back_rsem).wait()
    got = back_lse_recv.at[pl.ds(0, INNER - 1)]
    pltpu.make_async_copy(got, got, lse_rsem.at[0]).wait()
    mask = jnp.concatenate(diagonal(MID, 3, 0), axis=1)
    spread = half_sums(3 * 128)
    for p in range(PAIRS):
        first_row = (2 * p) % 8
        one = att_ref[p, pl.ds(first_row, MID, stride=8), :]
        two = att_ref[p, pl.ds(first_row + 1, MID, stride=8), :]
        lse1 = lse_ref[p]
        lse2 = jnp.where(mask, back_lse_recv[p], 0.0).astype(BF16)
        lse2 = jnp.dot(lse2, spread, preferred_element_type=F32)
        top = jnp.maximum(lse1, lse2)
        w1, w2 = jnp.exp(lse1 - top), jnp.exp(lse2 - top)
        total = w1 + w2
        merged = (w1 * jnp.where(second, two, one) + w2 * back_recv[p].astype(F32)) / total
        lse = top + jnp.log(total)
        for t in range(FAR):
            row = 32 * t + p // 4
            two_ref[0, 2 * p + t : 2 * p + t + 1, :] = merged[row : row + 1]
            two_ref[1, 2 * p + t : 2 * p + t + 1, :] = lse[row : row + 1]
        att_ref[p, pl.ds(first_row, MID, stride=8), :] = jnp.where(second, one, merged)
        att_ref[p, pl.ds(first_row + 1, MID, stride=8), :] = jnp.where(second, merged, two)
        merged_ref[:, 128 * p : 128 * p + 128] = att_ref[p, 0:ROWS, :].astype(BF16)

    sent = mid_send.at[pl.ds(0, INNER - 1)]
    pltpu.make_async_copy(sent, sent, mid_ssem).wait()
    sent = back_send.at[pl.ds(0, INNER - 1)]
    pltpu.make_async_copy(sent, sent, back_ssem).wait()
    sent = kv_recv.at[pl.ds(0, GG - 1)]
    pltpu.make_async_copy(sent, sent, kv_ssem).wait()
    sent = fq_recv.at[pl.ds(0, RG - 1)]
    pltpu.make_async_copy(sent, sent, fq_ssem).wait()
    sent = far_send.at[pl.ds(0, RG - 1)]
    pltpu.make_async_copy(sent, sent, far_ssem).wait()
    sent = back_lse_send.at[pl.ds(0, INNER - 1)]
    pltpu.make_async_copy(sent, sent, lse_ssem.at[0]).wait()
    sent = far_lse_send.at[pl.ds(0, RG - 1)]
    pltpu.make_async_copy(sent, sent, lse_ssem.at[1]).wait()

    got = far_recv.at[pl.ds(0, RG - 1)]
    pltpu.make_async_copy(got, got, far_rsem).wait()
    got = far_lse_recv.at[pl.ds(0, RG - 1)]
    pltpu.make_async_copy(got, got, lse_rsem.at[1]).wait()


def merge(merged_ref, two_ref, far_recv, far_lse_recv, out_hbm, edge, sem):
    copies = []
    for t in range(FAR):
        rest = pl.ds(256 * t + 16, 240)
        copies.append(pltpu.make_async_copy(merged_ref.at[rest, :], out_hbm.at[rest, :], sem.at[t]))
        copies[t].start()

    mask = diagonal(16, 3, 16)
    mask = jnp.logical_or(jnp.logical_or(mask[0], mask[1]), mask[2])
    partial_lse = jnp.concatenate([jnp.where(mask, far_lse_recv[s], 0.0) for s in range(RG)], axis=0).astype(BF16)
    partial_lse = jnp.dot(partial_lse, half_sums(128), preferred_element_type=F32)
    top = two_ref[1]
    for s in range(RG):
        top = jnp.maximum(top, partial_lse[16 * s : 16 * s + 16])
    weight = jnp.exp(two_ref[1] - top)
    numer = weight * two_ref[0]
    denom = weight
    for s in range(RG):
        weight = jnp.exp(partial_lse[16 * s : 16 * s + 16] - top)
        numer = numer + weight * far_recv[s].astype(F32)
        denom = denom + weight
    result = numer / denom

    row = lax.broadcasted_iota(jnp.int32, (16, 128), 0)
    half = lax.broadcasted_iota(jnp.int32, (16, 128), 1) // 64
    for t in range(FAR):
        for p in range(PAIRS):
            columns = slice(128 * p, 128 * p + 128)
            old = merged_ref[256 * t : 256 * t + 16, columns].astype(F32)
            new = jnp.where(row == 2 * p + half, result[2 * p + t : 2 * p + t + 1], old)
            edge[t, :, columns] = new.astype(BF16)
        copies.append(pltpu.make_async_copy(edge.at[t], out_hbm.at[pl.ds(256 * t, 16), :], sem.at[FAR + t]))
        copies[FAR + t].start()
    for copy in copies:
        copy.wait()


def on_device(queries, keys, values):
    dma = pltpu.SemaphoreType.DMA
    vmem = pltpu.VMEM
    results = pl.pallas_call(
        kernel,
        out_shape=[
            vmem((ROWS, 1024), BF16), vmem((2, 16, 128), F32), vmem((RG, 16, 128), BF16), vmem((RG, 1, 128), F32),
        ],
        in_specs=[pl.BlockSpec(memory_space=pltpu.HBM)] * 3,
        out_specs=[pl.BlockSpec(memory_space=pltpu.VMEM)] * 4,
        scratch_shapes=[
            vmem((ROWS, 1024), BF16), vmem((ROWS, 1024), BF16), vmem((ROWS, 1024), BF16),
            vmem((3, FAR, 16, 1024), BF16), dma((3,)), dma((3, FAR)),
            vmem((3, ROWS + 32, 128), F32), vmem((3, 16, 128), F32),
            vmem((INNER, 3 * MID, 128), BF16), vmem((INNER, 3 * MID, 128), BF16), dma, dma,
            vmem((INNER, MID, 128), BF16), vmem((INNER, MID, 128), BF16), dma, dma,
            vmem((INNER, 1, 384), F32), vmem((INNER, 1, 384), F32), vmem((RG, 1, 128), F32), dma((2,)), dma((2,)),
            vmem((32, 128), BF16), vmem((GG, 32, 128), BF16), dma, dma,
            vmem((16, 128), BF16), vmem((RG, 16, 128), BF16), dma, dma,
            vmem((RG, 16, 128), BF16), dma, dma,
            pltpu.SemaphoreType.REGULAR((2,)),
            vmem((PAIRS, ROWS + 8, 128), F32), vmem((ROWS + 8, 128), F32), vmem((PAIRS, MID, 128), F32),
            vmem((256 + 16, 128), F32), vmem((256 + 16, 128), F32),
        ],
        compiler_params=pltpu.CompilerParams(
            collective_id=0, has_side_effects=True, vmem_limit_bytes=40 * 1024 * 1024
        ),
    )(*(pltpu.with_memory_space_constraint(a, pltpu.HBM) for a in (queries, keys, values)))
    return pl.pallas_call(
        merge,
        out_shape=pltpu.HBM((ROWS, 1024), BF16),
        in_specs=[pl.BlockSpec(memory_space=pltpu.VMEM)] * 4,
        out_specs=pl.BlockSpec(memory_space=pltpu.HBM),
        scratch_shapes=[
            vmem((FAR, 16, 1024), BF16), dma((2 * FAR,)),
        ],
        compiler_params=pltpu.CompilerParams(vmem_limit_bytes=16 * 1024 * 1024),
    )(*(pltpu.with_memory_space_constraint(a, pltpu.VMEM) for a in results))


def solution(mesh):
    spec = P(("outer", "inner"), None)
    return jax.shard_map(
        on_device, mesh=mesh, in_specs=(spec, spec, spec), out_specs=spec, check_vma=False
    )
```
